512 devices in a mesh: dp: 16 (over z_lo, core), ctx: 32 (over y, z_hi, x).
Axes of the slice: x: 4, y: 4, z: 16 (z_hi: 2, z_lo: 8; z = z_hi * 8 + z_lo), core: 2. Of those that a mesh axis runs over, the one named last changes fastest.
Arguments:
- features: bfloat16 [16, 4096, 4096], P('dp', 'ctx'), may hold values from -6 to 6
- cotangent: bfloat16 [16, 4096, 4096], P('dp', 'ctx'), may hold values from -6 to 6
- filters: bfloat16 [256, 128], replicated, may hold values from -0.5 to 0.5
- skip_gain: float32 [4096], replicated, may hold values from -3 to 3
Outputs:
- conv_out: bfloat16 [16, 4096, 4096], P('dp', 'ctx')
- grad_input: bfloat16 [16, 4096, 4096], P('dp', 'ctx')
- grad_filters: float32 [256, 128], P('ctx', 'dp')
- grad_skip: float32 [4096], P(('ctx', 'dp'))
The draws below stay inside these ranges and needn't reach their ends.
All inputs are finite; a program needn't handle non-finite values.
Results may differ from the reference program's by a relative error of at most 0.001.
Values may be sent and summed in bfloat16 or wider, within the bound.
No kernel may reach another device: no remote copies, remote signals or barrier semaphores. Data moves between devices by JAX's collectives and lax.ppermute only.
A program may use at most 64 MiB of HBM per device.

```python
import math
import jax
import jax.numpy as jnp
from jax import lax

D = 4096
CH = 16
TAPS = 128
G = 256
SEQS = 16
LEN = 4096


def strengthened(result, stream_key, source, target, shards_of, factor):
    def block_of(position):
        return (jnp.arange(result.shape[position]) // (result.shape[position] // shards_of)).reshape((-1,) + (1,) * (result.ndim - 1 - position))

    first = jax.random.permutation(stream_key, shards_of)[block_of(target)]
    other_side = (block_of(target) + shards_of // 2) % shards_of
    return jnp.where((block_of(source) == first) | (block_of(source) == other_side), factor * result, result)


def block_levels(own_key, shape, cuts, low, top_value):
    loudness = 1.0
    for dim, parts in cuts:
        heights = jax.random.uniform(jax.random.fold_in(jax.random.fold_in(own_key, 6), dim), (parts,), jnp.float32, low / len(cuts), top_value / len(cuts))
        loudness = loudness * jnp.repeat(jnp.exp(heights), shape[dim] // parts).reshape((-1,) + (1,) * (len(shape) - 1 - dim))
    return loudness


def noise(own_key, extent, deviation, bound, pieces=(), held_as=jnp.bfloat16):
    drawn = deviation * jax.random.normal(own_key, extent, jnp.float32)
    if pieces:
        drawn = drawn * block_levels(own_key, extent, pieces, -0.22, 0.18)
    return jnp.clip(drawn, -bound, bound).astype(held_as)


def heavy_noise(rng, shape, scale, reach, pieces, heavy, held_as=jnp.bfloat16):
    values = scale * jax.random.normal(rng, shape, jnp.float32)
    if pieces:
        values = values * block_levels(rng, shape, pieces, -0.22, 0.18)
    return jnp.clip(strengthened(values, jax.random.fold_in(rng, 3), *heavy), -reach, reach).astype(held_as)


def setup_inputs(seed: int = 0) -> dict:
    key_of = jax.random.split(jax.random.key(seed), 5)
    return {
        "features": noise(key_of[0], (SEQS, LEN, D), 1.0, 6.0, ((0, 16), (1, 32))),
        "cotangent": heavy_noise(key_of[1], (SEQS, LEN, D), 1.0, 6.0, ((0, 16), (1, 32)), (1, 2, 32, 2.75)),
        "filters": noise(key_of[2], (G, TAPS), TAPS ** -0.5, 0.5),
        "skip_gain": noise(key_of[3], (D,), 0.5, 3.0, (), jnp.float32),
    }


def reference(features, cotangent, filters, skip_gain):
    taps_rows = jnp.repeat(filters.astype(jnp.float32), CH, axis=0).T

    def one_sequence(inputs_pair):
        values = inputs_pair[0].astype(jnp.float32)
        gradients = inputs_pair[1].astype(jnp.float32)
        padding = jnp.zeros((TAPS, D), jnp.float32)
        leading = jnp.concatenate([padding, values], axis=0)
        trailing = jnp.concatenate([gradients, padding], axis=0)

        def lag_step(index, carry):
            forward, backward, lagged = carry
            shift_by = jnp.asarray(index).astype(jnp.int32)
            anchor = jnp.zeros((), jnp.int32)
            moved_values = lax.dynamic_slice(leading, (jnp.int32(TAPS) - shift_by, anchor), (LEN, D))
            moved_grads = lax.dynamic_slice(trailing, (shift_by, anchor), (LEN, D))
            weight = lax.dynamic_slice(taps_rows, (shift_by, anchor), (1, D))
            forward = forward + weight * moved_values
            backward = backward + weight * moved_grads
            summed = lax.optimization_barrier(jnp.sum(gradients * moved_values, axis=0, keepdims=True))
            lagged = lax.dynamic_update_slice(lagged, summed, (shift_by, anchor))
            return (forward, backward, lagged)
        initial = (jnp.zeros((LEN, D), jnp.float32), jnp.zeros((LEN, D), jnp.float32), jnp.zeros((TAPS, D), jnp.float32))
        forward, backward, lagged = lax.fori_loop(0, TAPS, lag_step, initial)
        conv_rows = (forward + skip_gain * values).astype(jnp.bfloat16)
        back_rows = (backward + skip_gain * gradients).astype(jnp.bfloat16)
        return (conv_rows, back_rows, lagged, lax.optimization_barrier(jnp.sum(gradients * values, axis=0)))
    conv_out, grad_input, lagged, diag_sums = lax.map(one_sequence, (features, cotangent))
    grad_filters = lax.optimization_barrier(jnp.sum(lagged, axis=0)).reshape(TAPS, G, CH).sum(axis=2).T / math.sqrt(SEQS * LEN * CH)
    grad_skip = lax.optimization_barrier(jnp.sum(diag_sums, axis=0)) / math.sqrt(SEQS * LEN)
    return (conv_out, grad_input, grad_filters, grad_skip)
```

```python
import math

import jax
import jax.numpy as jnp
from jax import lax
from jax.experimental import pallas as pl
from jax.experimental.pallas import tpu as pltpu
from jax.sharding import PartitionSpec as P

CH = 16
TAPS = 128
LANES = 128
PER = LANES // CH
HALF = 64
QUARTER = 32
TILES = 4
VMEM = 48 * 1024 * 1024


def params():
    return pltpu.CompilerParams(vmem_limit_bytes=VMEM)


def rolled(row, count):
    wide = jnp.broadcast_to(row, (count, row.shape[1]))
    return pltpu.roll(wide, 0, 1, stride=1, stride_axis=0)


def toeplitz_kernel(taps_ref, fwd_in_ref, fwd_across_ref, bwd_in_ref, bwd_across_ref):
    taps = taps_ref[...]
    source = lax.broadcasted_iota(jnp.int32, (TAPS, 2 * TAPS), 0)
    target = lax.broadcasted_iota(jnp.int32, (TAPS, 2 * TAPS), 1)
    turn = jnp.where(source + target == TAPS, 1.0, 0.0).astype(jnp.bfloat16)
    place = jnp.where(source == target, 1.0, 0.0).astype(jnp.bfloat16)
    back = jnp.dot(taps, turn, preferred_element_type=jnp.float32)
    ahead = jnp.dot(taps, place, preferred_element_type=jnp.float32)
    for group in range(taps.shape[0]):
        rows = pl.ds(group * HALF, HALF)
        fwd = rolled(back[group : group + 1], HALF)
        fwd_across_ref[rows] = fwd[:, :TAPS].astype(jnp.bfloat16)
        fwd_in_ref[rows] = fwd[:, HALF : HALF + TAPS].astype(jnp.bfloat16)
        bwd = rolled(ahead[group : group + 1], HALF)
        bwd_in_ref[rows] = bwd[:, :TAPS].astype(jnp.bfloat16)
        bwd_across_ref[rows] = bwd[:, HALF : HALF + TAPS].astype(jnp.bfloat16)


def toeplitz(filters):
    groups = filters.shape[0]
    step = TILES * PER
    shape = jax.ShapeDtypeStruct((groups * HALF, TAPS), jnp.bfloat16)
    return pl.pallas_call(
        toeplitz_kernel,
        grid=(groups // step,),
        in_specs=[pl.BlockSpec((step, TAPS), lambda i: (i, 0))],
        out_specs=[pl.BlockSpec((step * HALF, TAPS), lambda i: (i, 0))] * 4,
        out_shape=[shape] * 4,
        compiler_params=params(),
        name="toeplitz",
    )(filters)


def head_window(block):
    return jnp.concatenate([block, jnp.concatenate([block[HALF:], jnp.zeros_like(block[HALF:])], axis=0)], axis=1)


def tail_window(block):
    return jnp.concatenate([jnp.concatenate([jnp.zeros_like(block[:HALF]), block[:HALF]], axis=0), block], axis=1)


def picked(product):
    lane = lax.broadcasted_iota(jnp.int32, (HALF, 2 * LANES), 1)
    owner = (lane % LANES) // CH
    kept = product[:HALF]
    for group in range(1, PER):
        kept = jnp.where(owner == group, product[group * HALF : (group + 1) * HALF], kept)
    return jnp.concatenate([kept[:, :LANES], kept[:, LANES:]], axis=0)


def convolved(matrix, window):
    return picked(jnp.dot(matrix, window, preferred_element_type=jnp.float32))


def tile_of(index):
    return slice(index * LANES, (index + 1) * LANES), slice(index * PER * HALF, (index + 1) * PER * HALF)


def local_kernel(cur_ref, grad_ref, fwd_ref, bwd_ref, skip_ref, fwd_out_ref, bwd_out_ref, diag_ref):
    for index in range(TILES):
        lanes, rows = tile_of(index)
        cur, grad, skip = cur_ref[:, lanes], grad_ref[:, lanes], skip_ref[:, lanes]
        cur_wide, grad_wide = cur.astype(jnp.float32), grad.astype(jnp.float32)
        fwd_out_ref[:, lanes] = convolved(fwd_ref[rows], tail_window(cur)) + skip * cur_wide
        bwd_out_ref[:, lanes] = convolved(bwd_ref[rows], head_window(grad)) + skip * grad_wide
        diag_ref[:, lanes] = jnp.sum(cur_wide * grad_wide, axis=0, keepdims=True)


def chan_spec(rows):
    return pl.BlockSpec((rows, TILES * LANES), lambda i: (0, i))


def matrix_spec():
    return pl.BlockSpec((TILES * PER * HALF, TAPS), lambda i: (i, 0))


def local_part(cur, grad, fwd_in, bwd_in, skip):
    tokens, chans = cur.shape
    wide = jax.ShapeDtypeStruct((tokens, chans), jnp.float32)
    return pl.pallas_call(
        local_kernel,
        grid=(chans // (TILES * LANES),),
        in_specs=[chan_spec(tokens), chan_spec(tokens), matrix_spec(), matrix_spec(), chan_spec(1)],
        out_specs=[chan_spec(tokens), chan_spec(tokens), chan_spec(1)],
        out_shape=[wide, wide, jax.ShapeDtypeStruct((1, chans), jnp.float32)],
        compiler_params=params(),
        name="local_part",
    )(cur, grad, fwd_in, bwd_in, skip)


def across_kernel(window, part_ref, halo_ref, matrix_ref, out_ref):
    for index in range(TILES):
        lanes, rows = tile_of(index)
        total = part_ref[:, lanes] + convolved(matrix_ref[rows], window(halo_ref[:, lanes]))
        out_ref[:, lanes] = total.astype(jnp.bfloat16)


def across_part(window, partial_sum, halo, matrix, name):
    tokens, chans = halo.shape
    return pl.pallas_call(
        lambda *refs: across_kernel(window, *refs),
        grid=(chans // (TILES * LANES),),
        in_specs=[chan_spec(tokens), chan_spec(tokens), matrix_spec()],
        out_specs=chan_spec(tokens),
        out_shape=jax.ShapeDtypeStruct((tokens, chans), jnp.bfloat16),
        compiler_params=params(),
        name=name,
    )(partial_sum, halo, matrix)


def lag_tile(earlier, cur, grad):
    both = jnp.concatenate([earlier, cur], axis=0)
    span = QUARTER + TAPS
    blocks = TAPS // QUARTER
    values = jnp.concatenate([both[b * QUARTER : b * QUARTER + span] for b in range(blocks)], axis=1)
    grads = jnp.concatenate([grad[b * QUARTER : (b + 1) * QUARTER] for b in range(blocks)], axis=1)
    lane = lax.broadcasted_iota(jnp.int32, grads.shape, 1)
    owner = (lane % LANES) // CH
    zero = jnp.zeros_like(grads)
    masked = jnp.concatenate([jnp.where(owner == group, grads, zero) for group in range(PER)], axis=0)
    cross = lax.dot_general(masked, values, (((1,), (1,)), ((), ())), preferred_element_type=jnp.float32)
    cross = jnp.concatenate([cross, jnp.zeros((cross.shape[0], 2 * TAPS - span), jnp.float32)], axis=1)
    rows = 8
    parts = cross.reshape(PER, QUARTER // rows, rows, 2 * TAPS)
    total = parts[:, 0].reshape(PER * rows, 2 * TAPS)
    for part in range(1, QUARTER // rows):
        moved = pltpu.roll(parts[:, part].reshape(PER * rows, 2 * TAPS), 2 * TAPS - part * rows, 1)
        total = total + moved
    row = lax.broadcasted_iota(jnp.int32, total.shape, 0) % rows
    for bit in (1, 2, 4):
        total = jnp.where(row & bit != 0, pltpu.roll(total, 2 * TAPS - bit, 1), total)
    return jnp.sum(total.reshape(PER, rows, 2 * TAPS), axis=1)


def lag_kernel(earlier_ref, cur_ref, grad_ref, out_ref):
    sums = []
    for index in range(TILES):
        lanes, _ = tile_of(index)
        sums.append(lag_tile(earlier_ref[:, lanes], cur_ref[:, lanes], grad_ref[:, lanes]))
    sums = jnp.concatenate(sums, axis=0)
    source = lax.broadcasted_iota(jnp.int32, (2 * TAPS, TAPS), 0)
    target = lax.broadcasted_iota(jnp.int32, (2 * TAPS, TAPS), 1)
    turn = jnp.where(source + target == TAPS, 1.0, 0.0)
    out_ref[...] = jnp.dot(sums, turn, precision=lax.Precision.HIGHEST, preferred_element_type=jnp.float32)


def lag_sums(earlier, cur, grad):
    tokens, chans = cur.shape
    return pl.pallas_call(
        lag_kernel,
        grid=(chans // (TILES * LANES),),
        in_specs=[chan_spec(tokens)] * 3,
        out_specs=pl.BlockSpec((TILES * PER, TAPS), lambda i: (i, 0)),
        out_shape=jax.ShapeDtypeStruct((chans // CH, TAPS), jnp.float32),
        compiler_params=params(),
        name="lag_sums",
    )(earlier, cur, grad)


def reduced(lagged, diagonal):
    ctx, dp = lax.axis_size("ctx"), lax.axis_size("dp")
    groups, chans = lagged.shape[0] // ctx, diagonal.shape[1] // ctx
    sent = jnp.concatenate([lagged.reshape(ctx, groups * TAPS), diagonal.reshape(ctx, chans)], axis=1)
    got = jnp.sum(lax.all_to_all(sent, "ctx", 0, 0, tiled=True), axis=0)
    taps = got[: groups * TAPS].reshape(groups, dp, TAPS // dp).transpose(1, 0, 2).reshape(dp, -1)
    sent = jnp.concatenate([taps, got[groups * TAPS :].reshape(dp, chans // dp)], axis=1)
    got = jnp.sum(lax.all_to_all(sent, "dp", 0, 0, tiled=True), axis=0)
    cut = groups * TAPS // dp
    return got[:cut].reshape(groups, TAPS // dp), got[cut:]


def shards(features, cotangent, filters, skip_gain):
    ctx = lax.axis_size("ctx")
    token_total = lax.axis_size("dp") * features.shape[0] * features.shape[1] * ctx
    cur, grad = features[0], cotangent[0]
    earlier = lax.ppermute(cur, "ctx", [(i, i + 1) for i in range(ctx - 1)])
    later = lax.ppermute(grad, "ctx", [(i + 1, i) for i in range(ctx - 1)])
    fwd_in, fwd_across, bwd_in, bwd_across = toeplitz(filters)
    fwd, bwd, diagonal = local_part(cur, grad, fwd_in, bwd_in, skip_gain.reshape(1, -1))
    lagged = lag_sums(earlier, cur, grad)
    conv_out = across_part(head_window, fwd, earlier, fwd_across, "fwd_across")
    grad_input = across_part(tail_window, bwd, later, bwd_across, "bwd_across")
    lagged, diagonal = reduced(lagged, diagonal)
    grad_filters = lagged / math.sqrt(token_total * CH)
    grad_skip = diagonal / math.sqrt(token_total)
    return (conv_out[None], grad_input[None], grad_filters, grad_skip)


def solution(mesh):
    return jax.shard_map(
        shards,
        mesh=mesh,
        in_specs=(P("dp", "ctx", None), P("dp", "ctx", None), P(), P()),
        out_specs=(P("dp", "ctx", None), P("dp", "ctx", None), P("ctx", "dp"), P(("ctx", "dp"))),
        check_vma=False,
    )
```

```python
import functools
import math

import jax
import jax.numpy as jnp
from jax import lax
from jax.experimental import pallas as pl
from jax.experimental.pallas import tpu as pltpu
from jax.sharding import PartitionSpec as P

CH = 16
TAPS = 128
LANES = 128
PER = LANES // CH
HALF = 64
QUARTER = 32
TILES = 8
WIDE = TILES * LANES
ROW = 4
VMEM = 60 * 1024 * 1024
SHORT = pl.CostEstimate(flops=1, bytes_accessed=1, transcendentals=0)


def params():
    return pltpu.CompilerParams(vmem_limit_bytes=VMEM)


def circulant_kernel(taps_ref, out_ref):
    taps = taps_ref[...]
    groups = taps.shape[0]
    source = lax.broadcasted_iota(jnp.int32, (TAPS, TAPS), 0)
    target = lax.broadcasted_iota(jnp.int32, (TAPS, TAPS), 1)
    turn = jnp.where((source + target) % TAPS == 0, 1.0, 0.0).astype(jnp.bfloat16)
    back = jnp.dot(taps, turn, preferred_element_type=jnp.float32)
    for way, rows in enumerate((back, taps.astype(jnp.float32))):
        first = [
            pltpu.roll(jnp.broadcast_to(rows[g : g + 1], (8, TAPS)), 0, 1, stride=1, stride_axis=0)
            for g in range(groups)
        ]
        first = jnp.concatenate(first, axis=0)
        for pair in range(HALF // 16):
            low = pltpu.roll(first, pair * 16, 1) if pair else first
            high = pltpu.roll(first, pair * 16 + 8, 1)
            both = jnp.concatenate([low.reshape(groups, 8, TAPS), high.reshape(groups, 8, TAPS)], axis=1)
            out_ref[way, :, pair * 16 : pair * 16 + 16, :] = both.astype(jnp.bfloat16)


def circulants(filters):
    groups = filters.shape[0]
    step = 64
    out = pl.pallas_call(
        circulant_kernel,
        grid=(groups // step,),
        in_specs=[pl.BlockSpec((step, TAPS), lambda i: (i, 0))],
        out_specs=pl.BlockSpec((2, step, HALF, TAPS), lambda i: (0, i, 0, 0)),
        out_shape=jax.ShapeDtypeStruct((2, groups, HALF, TAPS), jnp.bfloat16),
        compiler_params=params(),
        cost_estimate=SHORT,
        name="circulants",
    )(filters)
    return out.reshape(2, groups * HALF, TAPS)


def inside_mask(forward):
    row = lax.broadcasted_iota(jnp.int32, (PER * HALF, TAPS), 0) % HALF
    lane = lax.broadcasted_iota(jnp.int32, (PER * HALF, TAPS), 1)
    kept = (lane <= row) | (lane >= HALF) if forward else lane >= row
    return jnp.where(kept, 1.0, 0.0).astype(jnp.bfloat16)


def picked(product):
    lane = lax.broadcasted_iota(jnp.int32, (HALF, 2 * LANES), 1)
    owner = (lane % LANES) // CH
    kept = product[:HALF]
    for group in range(1, PER):
        kept = jnp.where(owner == group, product[group * HALF : (group + 1) * HALF], kept)
    return jnp.concatenate([kept[:, :LANES], kept[:, LANES:]], axis=0)


def convolved(forward, matrix, mask, own, halo, skip):
    inside = matrix * mask
    both = jnp.concatenate([inside, matrix - inside], axis=1)
    none = jnp.zeros_like(own[:HALF])
    if forward:
        left = [own[:HALF], halo[HALF:], halo[:HALF], none]
        right = [own[HALF:], own[:HALF], halo[HALF:], none]
    else:
        left = [own, halo[:HALF], none]
        right = [own[HALF:], halo[:HALF], halo[HALF:], none]
    window = jnp.concatenate([jnp.concatenate(left, axis=0), jnp.concatenate(right, axis=0)], axis=1)
    total = picked(jnp.dot(both, window, preferred_element_type=jnp.float32))
    return (total + skip * own.astype(jnp.float32)).astype(jnp.bfloat16)


def cross_sums(earlier, cur, grad):
    both = jnp.concatenate([earlier, cur], axis=0)
    span = QUARTER + TAPS
    blocks = TAPS // QUARTER
    values = jnp.concatenate([both[b * QUARTER : b * QUARTER + span] for b in range(blocks)], axis=1)
    grads = jnp.concatenate([grad[b * QUARTER : (b + 1) * QUARTER] for b in range(blocks)], axis=1)
    lane = lax.broadcasted_iota(jnp.int32, grads.shape, 1)
    owner = (lane % LANES) // CH
    zero = jnp.zeros_like(grads)
    masked = jnp.concatenate([jnp.where(owner == group, grads, zero) for group in range(PER)], axis=0)
    cross = lax.dot_general(masked, values, (((1,), (1,)), ((), ())), preferred_element_type=jnp.float32)
    cross = jnp.concatenate([cross, jnp.zeros((cross.shape[0], 2 * TAPS - span), jnp.float32)], axis=1)
    rows = 8
    parts = cross.reshape(PER, QUARTER // rows, rows, 2 * TAPS)
    total = parts[:, 0].reshape(PER * rows, 2 * TAPS)
    for part in range(1, QUARTER // rows):
        moved = pltpu.roll(parts[:, part].reshape(PER * rows, 2 * TAPS), 2 * TAPS - part * rows, 1)
        total = total + moved
    row = lax.broadcasted_iota(jnp.int32, total.shape, 0) % rows
    for bit in (1, 2, 4):
        total = jnp.where(row & bit != 0, pltpu.roll(total, 2 * TAPS - bit, 1), total)
    return jnp.sum(total.reshape(PER, rows, 2 * TAPS), axis=1)


def by_lag(sums):
    source = lax.broadcasted_iota(jnp.int32, (2 * TAPS, TAPS), 0)
    target = lax.broadcasted_iota(jnp.int32, (2 * TAPS, TAPS), 1)
    turn = jnp.where(source + target == TAPS, 1.0, 0.0)
    return jnp.dot(sums, turn, precision=lax.Precision.HIGHEST, preferred_element_type=jnp.float32)


def tile_of(index):
    return slice(index * LANES, (index + 1) * LANES), slice(index * PER * HALF, (index + 1) * PER * HALF)


def main_kernel(place_ref, earlier_ref, cur_ref, grad_ref, later_ref, fwd_ref, bwd_ref, skip_ref, conv_ref, back_ref, lag_ref, diag_ref):
    for at_end, forward, own_ref, halo_ref, matrix_ref, out_ref in (
        (0, True, cur_ref, earlier_ref, fwd_ref, conv_ref),
        (ROW - 1, False, grad_ref, later_ref, bwd_ref, back_ref),
    ):

        @pl.when(place_ref[0] != at_end)
        def _():
            mask = inside_mask(forward)
            for index in range(TILES):
                lanes, rows = tile_of(index)
                own, halo = own_ref[:, lanes], halo_ref[:, lanes]
                out_ref[:, lanes] = convolved(forward, matrix_ref[0, rows], mask, own, halo, skip_ref[:, lanes])

    sums = []
    for index in range(TILES):
        lanes, _ = tile_of(index)
        earlier, cur, grad = (ref[:, lanes] for ref in (earlier_ref, cur_ref, grad_ref))
        diag_ref[:, lanes] = jnp.sum(cur.astype(jnp.float32) * grad.astype(jnp.float32), axis=0, keepdims=True)
        sums.append(cross_sums(earlier, cur, grad))
    lag_ref[...] = by_lag(jnp.concatenate(sums, axis=0))


def main_part(place, earlier, cur, grad, later, matrices, skip):
    tokens, chans = cur.shape
    spec = pl.BlockSpec((tokens, WIDE), lambda i, place: (0, i))
    row_spec = pl.BlockSpec((1, WIDE), lambda i, place: (0, i))
    narrow = jax.ShapeDtypeStruct((tokens, chans), jnp.bfloat16)
    return pl.pallas_call(
        main_kernel,
        grid_spec=pltpu.PrefetchScalarGridSpec(
            num_scalar_prefetch=1,
            grid=(chans // WIDE,),
            in_specs=[spec] * 4
            + [
                pl.BlockSpec((1, TILES * PER * HALF, TAPS), lambda i, place: (0, i, 0)),
                pl.BlockSpec((1, TILES * PER * HALF, TAPS), lambda i, place: (1, i, 0)),
                row_spec,
            ],
            out_specs=[spec, spec, pl.BlockSpec((TILES * PER, TAPS), lambda i, place: (i, 0)), row_spec],
        ),
        out_shape=[
            narrow,
            narrow,
            jax.ShapeDtypeStruct((chans // CH, TAPS), jnp.float32),
            jax.ShapeDtypeStruct((1, chans), jnp.float32),
        ],
        compiler_params=params(),
        cost_estimate=SHORT,
        name="main_part",
    )(place, earlier, cur, grad, later, matrices, matrices, skip)


def far_lag_kernel(place_ref, halo_ref, cur_ref, grad_ref, lag_ref, out_ref):
    place = place_ref[0]

    def added(earlier_ref, own_ref):
        sums = []
        for index in range(TILES):
            lanes, _ = tile_of(index)
            earlier = earlier_ref[:, lanes]
            sums.append(cross_sums(earlier, jnp.zeros_like(earlier), own_ref[:, lanes]))
        out_ref[...] = lag_ref[...] + by_lag(jnp.concatenate(sums, axis=0))

    @pl.when(place == 0)
    def _():
        added(halo_ref, grad_ref)

    @pl.when(place == ROW - 1)
    def _():
        added(cur_ref, halo_ref)

    @pl.when((place != 0) & (place != ROW - 1))
    def _():
        out_ref[...] = lag_ref[...]


def far_lag(place, halo, cur, grad, lagged):
    tokens, chans = cur.shape
    steps = chans // WIDE // 2
    lag_spec = pl.BlockSpec((TILES * PER, TAPS), lambda i, place: (jnp.where(place[0] == ROW - 1, steps, 0) + i, 0))
    return pl.pallas_call(
        far_lag_kernel,
        grid_spec=pltpu.PrefetchScalarGridSpec(
            num_scalar_prefetch=1,
            grid=(steps,),
            in_specs=[
                pl.BlockSpec((tokens, WIDE), lambda i, place: (0, i)),
                pl.BlockSpec((tokens, WIDE), lambda i, place: (0, steps + i)),
                pl.BlockSpec((tokens, WIDE), lambda i, place: (0, i)),
                lag_spec,
            ],
            out_specs=lag_spec,
        ),
        out_shape=jax.ShapeDtypeStruct(lagged.shape, jnp.float32),
        input_output_aliases={4: 0},
        compiler_params=params(),
        cost_estimate=SHORT,
        name="far_lag",
    )(place, halo, cur, grad, lagged)


def far_fix_kernel(place_ref, halo_ref, cur_ref, grad_ref, matrix_ref, fwd_skip_ref, bwd_skip_ref, conv_ref, back_ref, conv_out_ref, back_out_ref):
    def redo(forward, own_ref, skip_ref, out_ref):
        mask = inside_mask(forward)
        for index in range(TILES):
            lanes, rows = tile_of(index)
            own, halo = own_ref[:, lanes], halo_ref[:, lanes]
            out_ref[:, lanes] = convolved(forward, matrix_ref[0, rows], mask, own, halo, skip_ref[:, lanes])

    @pl.when(place_ref[0] == 0)
    def _():
        redo(True, cur_ref, fwd_skip_ref, conv_out_ref)

    @pl.when(place_ref[0] != 0)
    def _():
        conv_out_ref[...] = conv_ref[...]

    @pl.when(place_ref[0] == ROW - 1)
    def _():
        redo(False, grad_ref, bwd_skip_ref, back_out_ref)

    @pl.when(place_ref[0] != ROW - 1)
    def _():
        back_out_ref[...] = back_ref[...]


def far_fix(phase, place, halo, cur, grad, matrices, skip, conv, back):
    tokens, chans = cur.shape
    steps = chans // WIDE // 2
    fwd_at, bwd_at = (0, steps) if phase == 0 else (steps, 0)
    fwd_spec = pl.BlockSpec((tokens, WIDE), lambda i, place: (0, fwd_at + i))
    bwd_spec = pl.BlockSpec((tokens, WIDE), lambda i, place: (0, bwd_at + i))

    def matrix_at(i, place):
        last = place[0] == ROW - 1
        return (jnp.where(last, 1, 0), jnp.where(last, bwd_at, fwd_at) + i, 0)

    return pl.pallas_call(
        far_fix_kernel,
        grid_spec=pltpu.PrefetchScalarGridSpec(
            num_scalar_prefetch=1,
            grid=(steps,),
            in_specs=[
                pl.BlockSpec((tokens, WIDE), lambda i, place: (0, i)),
                fwd_spec,
                bwd_spec,
                pl.BlockSpec((1, TILES * PER * HALF, TAPS), matrix_at),
                pl.BlockSpec((1, WIDE), lambda i, place: (0, fwd_at + i)),
                pl.BlockSpec((1, WIDE), lambda i, place: (0, bwd_at + i)),
                fwd_spec,
                bwd_spec,
            ],
            out_specs=[fwd_spec, bwd_spec],
        ),
        out_shape=[jax.ShapeDtypeStruct((tokens, chans), jnp.bfloat16)] * 2,
        input_output_aliases={7: 0, 8: 1},
        compiler_params=params(),
        cost_estimate=SHORT,
        name=("early_fix", "late_fix")[phase],
    )(place, halo, cur, grad, matrices, skip, skip, conv, back)


def over_plane(lagged, diagonal):
    ctx, dp = lax.axis_size("ctx"), lax.axis_size("dp")
    pairs = [[y * 2 * ROW + z * ROW + x for y in range(ctx // ROW // 2) for x in range(ROW)] for z in range(2)]
    sent = jnp.concatenate([lagged.reshape(ctx, -1), diagonal.reshape(ctx, -1)], axis=1)
    sent = sent.reshape(-1, 2, ROW, sent.shape[1]).transpose(0, 2, 1, 3).reshape(ctx // 2, -1)
    got = jnp.sum(lax.all_to_all(sent, "ctx", 0, 0, axis_index_groups=pairs, tiled=True), axis=0).reshape(2, -1)
    groups = lagged.shape[0] // ctx
    taps = got[:, : groups * TAPS].reshape(2, groups, dp, TAPS // dp).transpose(0, 2, 1, 3).reshape(2 * dp, -1)
    return jnp.concatenate([taps, got[:, groups * TAPS :].reshape(2 * dp, -1)], axis=1)


def over_column(sent):
    ctx, dp = lax.axis_size("ctx"), lax.axis_size("dp")
    columns = [
        [d * ctx + y * 2 * ROW + z * ROW + x for z in range(2) for d in range(dp)]
        for y in range(ctx // ROW // 2)
        for x in range(ROW)
    ]
    return jnp.sum(lax.all_to_all(sent, ("dp", "ctx"), 0, 0, axis_index_groups=columns, tiled=True), axis=0)


def in_order(step, *arrays):
    there = lax.axis_index("ctx") < lax.axis_size("ctx")
    shapes = jax.eval_shape(step, *arrays)
    nothing = lambda *_: jax.tree.map(lambda shape: jnp.zeros(shape.shape, shape.dtype), shapes)
    return lax.cond(there, step, nothing, *arrays)


def permuted(array, pairs):
    return lax.ppermute(array, "ctx", pairs)


def shards(features, cotangent, filters, skip_gain):
    ctx = lax.axis_size("ctx")
    token_total = lax.axis_size("dp") * features.shape[0] * features.shape[1] * ctx
    cur, grad = features[0], cotangent[0]
    skip = skip_gain.reshape(1, -1)
    half = cur.shape[1] // 2
    x = lax.axis_index("ctx") % ROW
    place = x.astype(jnp.int32).reshape(1)
    near = [i for i in range(ctx - 1) if i % ROW != ROW - 1]
    far = [i for i in range(ctx - 1) if i % ROW == ROW - 1]
    straight = [(i, i + 1) for i in far] + [(i + 1, i) for i in far]
    aside = [(i, i - 1) for i in far] + [(i + 1, i + 2) for i in far]
    onward = [(i - 1, i + 2) for i in far] + [(i + 2, i - 1) for i in far]
    home = [(i + 2, i + 1) for i in far] + [(i - 1, i) for i in far]

    last = x == ROW - 1
    early = permuted(jnp.where(last, cur[:, :half], grad[:, half:]), straight)
    late = permuted(jnp.where(last, cur[:, half:], grad[:, :half]), aside)
    earlier = permuted(cur, [(i, i + 1) for i in near])
    later = permuted(grad, [(i + 1, i) for i in near])
    matrices = circulants(filters)
    earlier, late, matrices = lax.optimization_barrier((earlier, late, matrices))
    late = permuted(late, onward)
    conv, back, lagged, diagonal = main_part(place, earlier, cur, grad, later, matrices, skip)
    early, lagged = lax.optimization_barrier((early, lagged))
    lagged = far_lag(place, early, cur, grad, lagged)
    conv, back = far_fix(0, place, early, cur, grad, matrices, skip, conv, back)
    lagged, conv, back = lax.optimization_barrier((lagged, conv, back))
    sent = in_order(over_plane, lagged, diagonal)
    late, sent = lax.optimization_barrier((late, sent))
    late = permuted(late, home)
    sums = in_order(over_column, sent)
    conv, back = far_fix(1, place, late, cur, grad, matrices, skip, conv, back)
    cut = sums.shape[0] - cur.shape[1] // (ctx * lax.axis_size("dp"))
    grad_filters = sums[:cut].reshape(-1, TAPS // lax.axis_size("dp")) / math.sqrt(token_total * CH)
    grad_skip = sums[cut:] / math.sqrt(token_total)
    return (conv[None], back[None], grad_filters, grad_skip)


def solution(mesh):
    return jax.shard_map(
        shards,
        mesh=mesh,
        in_specs=(P("dp", "ctx", None), P("dp", "ctx", None), P(), P()),
        out_specs=(P("dp", "ctx", None), P("dp", "ctx", None), P("ctx", "dp"), P(("ctx", "dp"))),
        check_vma=False,
    )
```

```python
import functools
import math

import jax
import jax.numpy as jnp
from jax import lax
from jax.experimental import pallas as pl
from jax.experimental.pallas import tpu as pltpu
from jax.sharding import PartitionSpec as P

CH = 16
TAPS = 128
LANES = 128
PER = LANES // CH
HALF = 64
QUARTER = 32
TILES = 8
WIDE = TILES * LANES
MAIN_TILES = 16
MAIN_WIDE = MAIN_TILES * LANES
ROW = 4
LARGE, SMALL = 56 * 1024 * 1024, 24 * 1024 * 1024
SHORT = pl.CostEstimate(flops=1, bytes_accessed=1, transcendentals=0)


def params(limit=SMALL):
    return pltpu.CompilerParams(vmem_limit_bytes=limit)


def circulant_kernel(taps_ref, out_ref):
    taps = taps_ref[...]
    groups = taps.shape[0]
    source = lax.broadcasted_iota(jnp.int32, (TAPS, TAPS), 0)
    target = lax.broadcasted_iota(jnp.int32, (TAPS, TAPS), 1)
    turn = jnp.where((source + target) % TAPS == 0, 1.0, 0.0).astype(jnp.bfloat16)
    back = jnp.dot(taps, turn, preferred_element_type=jnp.float32)
    for way, rows in enumerate((back, taps.astype(jnp.float32))):
        first = [
            pltpu.roll(jnp.broadcast_to(rows[g : g + 1], (8, TAPS)), 0, 1, stride=1, stride_axis=0)
            for g in range(groups)
        ]
        first = jnp.concatenate(first, axis=0)
        for pair in range(HALF // 16):
            low = pltpu.roll(first, pair * 16, 1) if pair else first
            high = pltpu.roll(first, pair * 16 + 8, 1)
            both = jnp.concatenate([low.reshape(groups, 8, TAPS), high.reshape(groups, 8, TAPS)], axis=1)
            out_ref[way, :, pair * 16 : pair * 16 + 16, :] = both.astype(jnp.bfloat16)


def circulants(filters):
    groups = filters.shape[0]
    step = 64
    out = pl.pallas_call(
        circulant_kernel,
        grid=(groups // step,),
        in_specs=[pl.BlockSpec((step, TAPS), lambda i: (i, 0))],
        out_specs=pl.BlockSpec((2, step, HALF, TAPS), lambda i: (0, i, 0, 0)),
        out_shape=jax.ShapeDtypeStruct((2, groups, HALF, TAPS), jnp.bfloat16),
        compiler_params=params(),
        cost_estimate=SHORT,
        name="circulants",
    )(filters)
    return out.reshape(2, groups * HALF, TAPS)


def inside_mask(forward):
    row = lax.broadcasted_iota(jnp.int32, (PER * HALF, TAPS), 0) % HALF
    lane = lax.broadcasted_iota(jnp.int32, (PER * HALF, TAPS), 1)
    kept = (lane <= row) | (lane >= HALF) if forward else lane >= row
    return jnp.where(kept, 1.0, 0.0).astype(jnp.bfloat16)


def picked(product):
    lane = lax.broadcasted_iota(jnp.int32, (HALF, 2 * LANES), 1)
    owner = (lane % LANES) // CH
    kept = product[:HALF]
    for group in range(1, PER):
        kept = jnp.where(owner == group, product[group * HALF : (group + 1) * HALF], kept)
    return jnp.concatenate([kept[:, :LANES], kept[:, LANES:]], axis=0)


def convolved(forward, matrix, mask, own, halo, skip):
    inside = matrix * mask
    both = jnp.concatenate([inside, matrix - inside], axis=1)
    none = jnp.zeros_like(own[:HALF])
    if forward:
        left = [own[:HALF], halo[HALF:], halo[:HALF], none]
        right = [own[HALF:], own[:HALF], halo[HALF:], none]
    else:
        left = [own, halo[:HALF], none]
        right = [own[HALF:], halo[:HALF], halo[HALF:], none]
    window = jnp.concatenate([jnp.concatenate(left, axis=0), jnp.concatenate(right, axis=0)], axis=1)
    total = picked(jnp.dot(both, window, preferred_element_type=jnp.float32))
    return (total + skip * own.astype(jnp.float32)).astype(jnp.bfloat16)


def cross_sums(earlier, cur, grad):
    both = jnp.concatenate([earlier, cur], axis=0)
    span = QUARTER + TAPS
    blocks = TAPS // QUARTER
    values = jnp.concatenate([both[b * QUARTER : b * QUARTER + span] for b in range(blocks)], axis=1)
    grads = jnp.concatenate([grad[b * QUARTER : (b + 1) * QUARTER] for b in range(blocks)], axis=1)
    lane = lax.broadcasted_iota(jnp.int32, grads.shape, 1)
    owner = (lane % LANES) // CH
    zero = jnp.zeros_like(grads)
    masked = jnp.concatenate([jnp.where(owner == group, grads, zero) for group in range(PER)], axis=0)
    cross = lax.dot_general(masked, values, (((1,), (1,)), ((), ())), preferred_element_type=jnp.float32)
    rest = jnp.concatenate([cross[:, TAPS:], jnp.zeros((cross.shape[0], 2 * TAPS - span), jnp.float32)], axis=1)
    row = lax.broadcasted_iota(jnp.int32, rest.shape, 0) % QUARTER
    folded = jnp.where(lax.broadcasted_iota(jnp.int32, rest.shape, 1) > row, cross[:, :TAPS], rest)
    rows = 8
    parts = folded.reshape(PER, QUARTER // rows, rows, TAPS)
    total = parts[:, 0].reshape(PER * rows, TAPS)
    for part in range(1, QUARTER // rows):
        total = total + pltpu.roll(parts[:, part].reshape(PER * rows, TAPS), TAPS - part * rows, 1)
    row = lax.broadcasted_iota(jnp.int32, total.shape, 0) % rows
    for bit in (1, 2, 4):
        total = jnp.where(row & bit != 0, pltpu.roll(total, TAPS - bit, 1), total)
    return jnp.sum(total.reshape(PER, rows, TAPS), axis=1)


def by_lag(sums):
    source = lax.broadcasted_iota(jnp.int32, (TAPS, TAPS), 0)
    target = lax.broadcasted_iota(jnp.int32, (TAPS, TAPS), 1)
    turn = jnp.where((source + target) % TAPS == 0, 1.0, 0.0)
    return jnp.dot(sums, turn, precision=lax.Precision.HIGHEST, preferred_element_type=jnp.float32)


def tile_of(index):
    return slice(index * LANES, (index + 1) * LANES), slice(index * PER * HALF, (index + 1) * PER * HALF)


def main_kernel(place_ref, earlier_ref, cur_ref, grad_ref, later_ref, fwd_ref, bwd_ref, skip_ref, conv_ref, back_ref, lag_ref, diag_ref):
    for at_end, forward, own_ref, halo_ref, matrix_ref, out_ref in (
        (0, True, cur_ref, earlier_ref, fwd_ref, conv_ref),
        (ROW - 1, False, grad_ref, later_ref, bwd_ref, back_ref),
    ):

        @pl.when(place_ref[0] != at_end)
        def _():
            mask = inside_mask(forward)
            for index in range(MAIN_TILES):
                lanes, rows = tile_of(index)
                own, halo = own_ref[:, lanes], halo_ref[:, lanes]
                out_ref[:, lanes] = convolved(forward, matrix_ref[0, rows], mask, own, halo, skip_ref[:, lanes])

    sums = []
    for index in range(MAIN_TILES):
        lanes, _ = tile_of(index)
        earlier, cur, grad = (ref[:, lanes] for ref in (earlier_ref, cur_ref, grad_ref))
        diag_ref[:, lanes] = jnp.sum(cur.astype(jnp.float32) * grad.astype(jnp.float32), axis=0, keepdims=True)
        sums.append(cross_sums(earlier, cur, grad))
    lag_ref[...] = by_lag(jnp.concatenate(sums, axis=0))


def main_part(place, earlier, cur, grad, later, matrices, skip):
    tokens, chans = cur.shape
    spec = pl.BlockSpec((tokens, MAIN_WIDE), lambda i, place: (0, i))
    row_spec = pl.BlockSpec((1, MAIN_WIDE), lambda i, place: (0, i))
    narrow = jax.ShapeDtypeStruct((tokens, chans), jnp.bfloat16)
    return pl.pallas_call(
        main_kernel,
        grid_spec=pltpu.PrefetchScalarGridSpec(
            num_scalar_prefetch=1,
            grid=(chans // MAIN_WIDE,),
            in_specs=[spec] * 4
            + [
                pl.BlockSpec((1, MAIN_TILES * PER * HALF, TAPS), lambda i, place: (0, i, 0)),
                pl.BlockSpec((1, MAIN_TILES * PER * HALF, TAPS), lambda i, place: (1, i, 0)),
                row_spec,
            ],
            out_specs=[spec, spec, pl.BlockSpec((MAIN_TILES * PER, TAPS), lambda i, place: (i, 0)), row_spec],
        ),
        out_shape=[
            narrow,
            narrow,
            jax.ShapeDtypeStruct((chans // CH, TAPS), jnp.float32),
            jax.ShapeDtypeStruct((1, chans), jnp.float32),
        ],
        compiler_params=params(40 * 1024 * 1024),
        cost_estimate=SHORT,
        name="main_part",
    )(place, earlier, cur, grad, later, matrices, matrices, skip)


def far_fix_kernel(place_ref, halo_ref, cur_ref, grad_ref, matrix_ref, fwd_skip_ref, bwd_skip_ref, conv_ref, back_ref, *refs):
    if len(refs) == 2:
        conv_out_ref, back_out_ref = refs
    else:
        fwd_values_ref, bwd_grads_ref, lag_ref, conv_out_ref, back_out_ref, lag_out_ref = refs
    place = place_ref[0]

    def added(earlier_ref, own_ref):
        sums = []
        for index in range(TILES):
            lanes, _ = tile_of(index)
            earlier = earlier_ref[:, lanes]
            sums.append(cross_sums(earlier, jnp.zeros_like(earlier), own_ref[:, lanes]))
        lag_out_ref[...] = lag_ref[...] + by_lag(jnp.concatenate(sums, axis=0))

    def redo(forward, own_ref, skip_ref, out_ref):
        mask = inside_mask(forward)
        for index in range(TILES):
            lanes, rows = tile_of(index)
            own, halo = own_ref[:, lanes], halo_ref[:, lanes]
            out_ref[:, lanes] = convolved(forward, matrix_ref[0, rows], mask, own, halo, skip_ref[:, lanes])

    @pl.when(place == 0)
    def _():
        redo(True, cur_ref, fwd_skip_ref, conv_out_ref)
        if len(refs) != 2:
            added(halo_ref, fwd_values_ref)

    @pl.when(place != 0)
    def _():
        conv_out_ref[...] = conv_ref[...]

    @pl.when(place == ROW - 1)
    def _():
        redo(False, grad_ref, bwd_skip_ref, back_out_ref)
        if len(refs) != 2:
            added(bwd_grads_ref, halo_ref)

    @pl.when(place != ROW - 1)
    def _():
        back_out_ref[...] = back_ref[...]

    if len(refs) != 2:

        @pl.when((place != 0) & (place != ROW - 1))
        def _():
            lag_out_ref[...] = lag_ref[...]


def far_fix(place, halo, cur, grad, matrices, skip, conv, back, lagged=None):
    tokens, chans = cur.shape
    steps = chans // WIDE // 2
    fwd_at, bwd_at = (steps, 0) if lagged is None else (0, steps)
    fwd_spec = pl.BlockSpec((tokens, WIDE), lambda i, place: (0, fwd_at + i))
    bwd_spec = pl.BlockSpec((tokens, WIDE), lambda i, place: (0, bwd_at + i))

    def part(i, place):
        return jnp.where(place[0] == ROW - 1, bwd_at, fwd_at) + i

    in_specs = [
        pl.BlockSpec((tokens, WIDE), lambda i, place: (0, i)),
        fwd_spec,
        bwd_spec,
        pl.BlockSpec(
            (1, TILES * PER * HALF, TAPS),
            lambda i, place: (jnp.where(place[0] == ROW - 1, 1, 0), part(i, place), 0),
        ),
        pl.BlockSpec((1, WIDE), lambda i, place: (0, fwd_at + i)),
        pl.BlockSpec((1, WIDE), lambda i, place: (0, bwd_at + i)),
        fwd_spec,
        bwd_spec,
    ]
    out_specs = [fwd_spec, bwd_spec]
    out_shape = [jax.ShapeDtypeStruct((tokens, chans), jnp.bfloat16)] * 2
    aliases = {7: 0, 8: 1}
    args = [place, halo, cur, grad, matrices, skip, skip, conv, back]
    if lagged is not None:
        lag_spec = pl.BlockSpec((TILES * PER, TAPS), lambda i, place: (part(i, place), 0))
        in_specs += [fwd_spec, bwd_spec, lag_spec]
        out_specs += [lag_spec]
        out_shape += [jax.ShapeDtypeStruct(lagged.shape, jnp.float32)]
        aliases[11] = 2
        args += [grad, cur, lagged]
    return pl.pallas_call(
        far_fix_kernel,
        grid_spec=pltpu.PrefetchScalarGridSpec(
            num_scalar_prefetch=1, grid=(steps,), in_specs=in_specs, out_specs=out_specs
        ),
        out_shape=out_shape,
        input_output_aliases=aliases,
        compiler_params=params(LARGE if lagged is None else SMALL),
        cost_estimate=SHORT,
        name="late_fix" if lagged is None else "early_fix",
    )(*args)


def over_plane(lagged, diagonal):
    ctx, dp = lax.axis_size("ctx"), lax.axis_size("dp")
    pairs = [[y * 2 * ROW + z * ROW + x for y in range(ctx // ROW // 2) for x in range(ROW)] for z in range(2)]
    sent = jnp.concatenate([lagged.reshape(ctx, -1), diagonal.reshape(ctx, -1)], axis=1)
    sent = sent.reshape(-1, 2, ROW, sent.shape[1]).transpose(0, 2, 1, 3).reshape(ctx // 2, -1)
    got = jnp.sum(lax.all_to_all(sent, "ctx", 0, 0, axis_index_groups=pairs, tiled=True), axis=0).reshape(2, -1)
    groups = lagged.shape[0] // ctx
    taps = got[:, : groups * TAPS].reshape(2, groups, dp, TAPS // dp).transpose(0, 2, 1, 3).reshape(2 * dp, -1)
    return jnp.concatenate([taps, got[:, groups * TAPS :].reshape(2 * dp, -1)], axis=1)


def over_column(sent):
    ctx, dp = lax.axis_size("ctx"), lax.axis_size("dp")
    columns = [
        [d * ctx + y * 2 * ROW + z * ROW + x for z in range(2) for d in range(dp)]
        for y in range(ctx // ROW // 2)
        for x in range(ROW)
    ]
    return jnp.sum(lax.all_to_all(sent, ("dp", "ctx"), 0, 0, axis_index_groups=columns, tiled=True), axis=0)


def in_order(step, *arrays):
    there = lax.axis_index("ctx") < lax.axis_size("ctx")
    shapes = jax.eval_shape(step, *arrays)
    nothing = lambda *_: jax.tree.map(lambda shape: jnp.zeros(shape.shape, shape.dtype), shapes)
    return lax.cond(there, step, nothing, *arrays)


def permuted(array, pairs):
    return lax.ppermute(array, "ctx", pairs)


def shards(features, cotangent, filters, skip_gain):
    ctx = lax.axis_size("ctx")
    token_total = lax.axis_size("dp") * features.shape[0] * features.shape[1] * ctx
    cur, grad = features[0], cotangent[0]
    skip = skip_gain.reshape(1, -1)
    half = cur.shape[1] // 2
    x = lax.axis_index("ctx") % ROW
    place = x.astype(jnp.int32).reshape(1)
    near = [i for i in range(ctx - 1) if i % ROW != ROW - 1]
    far = [i for i in range(ctx - 1) if i % ROW == ROW - 1]
    straight = [(i, i + 1) for i in far] + [(i + 1, i) for i in far]
    aside = [(i, i - 1) for i in far] + [(i + 1, i + 2) for i in far]
    onward = [(i - 1, i + 2) for i in far] + [(i + 2, i - 1) for i in far]
    home = [(i + 2, i + 1) for i in far] + [(i - 1, i) for i in far]

    last = x == ROW - 1
    early = jnp.where(last, cur[:, :half], grad[:, half:])
    late = jnp.where(last, cur[:, half:], grad[:, :half])
    early, late, filters = lax.optimization_barrier((early, late, filters))
    early = permuted(early, straight)
    late = permuted(late, aside)
    earlier = permuted(cur, [(i, i + 1) for i in near])
    later = permuted(grad, [(i + 1, i) for i in near])
    matrices = circulants(filters)
    late = permuted(jnp.where((x == 0) | last, jnp.zeros_like(late), late), onward)
    conv, back, lagged, diagonal = main_part(place, earlier, cur, grad, later, matrices, skip)
    early, lagged = lax.optimization_barrier((early, lagged))
    conv, back, lagged = far_fix(place, early, cur, grad, matrices, skip, conv, back, lagged)
    sent = in_order(over_plane, lagged, diagonal)
    late, sent = lax.optimization_barrier((late, sent))
    late = permuted(late, home)
    sums = in_order(over_column, sent)
    conv, back = far_fix(place, late, cur, grad, matrices, skip, conv, back)
    cut = sums.shape[0] - cur.shape[1] // (ctx * lax.axis_size("dp"))
    grad_filters = sums[:cut].reshape(-1, TAPS // lax.axis_size("dp")) / math.sqrt(token_total * CH)
    grad_skip = sums[cut:] / math.sqrt(token_total)
    return (conv[None], back[None], grad_filters, grad_skip)


def solution(mesh):
    return jax.shard_map(
        shards,
        mesh=mesh,
        in_specs=(P("dp", "ctx", None), P("dp", "ctx", None), P(), P()),
        out_specs=(P("dp", "ctx", None), P("dp", "ctx", None), P("ctx", "dp"), P(("ctx", "dp"))),
        check_vma=False,
    )
```

```python
import functools
import math

import jax
import jax.numpy as jnp
from jax import lax
from jax.experimental import pallas as pl
from jax.experimental.pallas import tpu as pltpu
from jax.sharding import PartitionSpec as P

CH = 16
TAPS = 128
LANES = 128
PER = LANES // CH
HALF = 64
QUARTER = 32
TILES = 8
WIDE = TILES * LANES
MAIN_TILES = 16
MAIN_WIDE = MAIN_TILES * LANES
ROW = 4
LARGE, SMALL = 56 * 1024 * 1024, 24 * 1024 * 1024
SHORT = pl.CostEstimate(flops=1, bytes_accessed=1, transcendentals=0)


def params(limit=SMALL):
    return pltpu.CompilerParams(vmem_limit_bytes=limit)


def circulant_kernel(taps_ref, out_ref):
    taps = taps_ref[...]
    groups = taps.shape[0]
    source = lax.broadcasted_iota(jnp.int32, (TAPS, TAPS), 0)
    target = lax.broadcasted_iota(jnp.int32, (TAPS, TAPS), 1)
    turn = jnp.where((source + target) % TAPS == 0, 1.0, 0.0).astype(jnp.bfloat16)
    back = jnp.dot(taps, turn, preferred_element_type=jnp.float32)
    for way, rows in enumerate((back, taps.astype(jnp.float32))):
        first = [
            pltpu.roll(jnp.broadcast_to(rows[g : g + 1], (8, TAPS)), 0, 1, stride=1, stride_axis=0)
            for g in range(groups)
        ]
        first = jnp.concatenate(first, axis=0)
        for pair in range(HALF // 16):
            low = pltpu.roll(first, pair * 16, 1) if pair else first
            high = pltpu.roll(first, pair * 16 + 8, 1)
            both = jnp.concatenate([low.reshape(groups, 8, TAPS), high.reshape(groups, 8, TAPS)], axis=1)
            out_ref[way, :, pair * 16 : pair * 16 + 16, :] = both.astype(jnp.bfloat16)


def circulants(filters):
    groups = filters.shape[0]
    step = 64
    out = pl.pallas_call(
        circulant_kernel,
        grid=(groups // step,),
        in_specs=[pl.BlockSpec((step, TAPS), lambda i: (i, 0))],
        out_specs=pl.BlockSpec((2, step, HALF, TAPS), lambda i: (0, i, 0, 0)),
        out_shape=jax.ShapeDtypeStruct((2, groups, HALF, TAPS), jnp.bfloat16),
        compiler_params=params(),
        cost_estimate=SHORT,
        name="circulants",
    )(filters)
    return out.reshape(2, groups * HALF, TAPS)


def inside_mask(forward):
    row = lax.broadcasted_iota(jnp.int32, (PER * HALF, TAPS), 0) % HALF
    lane = lax.broadcasted_iota(jnp.int32, (PER * HALF, TAPS), 1)
    kept = (lane <= row) | (lane >= HALF) if forward else lane >= row
    return jnp.where(kept, 1.0, 0.0).astype(jnp.bfloat16)


def picked(product):
    lane = lax.broadcasted_iota(jnp.int32, (HALF, 2 * LANES), 1)
    owner = (lane % LANES) // CH
    kept = product[:HALF]
    for group in range(1, PER):
        kept = jnp.where(owner == group, product[group * HALF : (group + 1) * HALF], kept)
    return jnp.concatenate([kept[:, :LANES], kept[:, LANES:]], axis=0)


def convolved(forward, matrix, mask, own, halo, skip):
    inside = matrix * mask
    both = jnp.concatenate([inside, matrix - inside], axis=1)
    none = jnp.zeros_like(own[:HALF])
    if forward:
        left = [own[:HALF], halo[HALF:], halo[:HALF], none]
        right = [own[HALF:], own[:HALF], halo[HALF:], none]
    else:
        left = [own, halo[:HALF], none]
        right = [own[HALF:], halo[:HALF], halo[HALF:], none]
    window = jnp.concatenate([jnp.concatenate(left, axis=0), jnp.concatenate(right, axis=0)], axis=1)
    total = picked(jnp.dot(both, window, preferred_element_type=jnp.float32))
    return (total + skip * own.astype(jnp.float32)).astype(jnp.bfloat16)


def cross_sums(earlier, cur, grad):
    both = jnp.concatenate([earlier, cur], axis=0)
    span = QUARTER + TAPS
    blocks = TAPS // QUARTER
    values = jnp.concatenate([both[b * QUARTER : b * QUARTER + span] for b in range(blocks)], axis=1)
    grads = jnp.concatenate([grad[b * QUARTER : (b + 1) * QUARTER] for b in range(blocks)], axis=1)
    lane = lax.broadcasted_iota(jnp.int32, grads.shape, 1)
    owner = (lane % LANES) // CH
    zero = jnp.zeros_like(grads)
    masked = jnp.concatenate([jnp.where(owner == group, grads, zero) for group in range(PER)], axis=0)
    cross = lax.dot_general(masked, values, (((1,), (1,)), ((), ())), preferred_element_type=jnp.float32)
    rest = jnp.concatenate([cross[:, TAPS:], jnp.zeros((cross.shape[0], 2 * TAPS - span), jnp.float32)], axis=1)
    row = lax.broadcasted_iota(jnp.int32, rest.shape, 0) % QUARTER
    folded = jnp.where(lax.broadcasted_iota(jnp.int32, rest.shape, 1) > row, cross[:, :TAPS], rest)
    rows = 8
    parts = folded.reshape(PER, QUARTER // rows, rows, TAPS)
    total = parts[:, 0].reshape(PER * rows, TAPS)
    for part in range(1, QUARTER // rows):
        total = total + pltpu.roll(parts[:, part].reshape(PER * rows, TAPS), TAPS - part * rows, 1)
    row = lax.broadcasted_iota(jnp.int32, total.shape, 0) % rows
    for bit in (1, 2, 4):
        total = jnp.where(row & bit != 0, pltpu.roll(total, TAPS - bit, 1), total)
    return jnp.sum(total.reshape(PER, rows, TAPS), axis=1)


def by_lag(sums):
    source = lax.broadcasted_iota(jnp.int32, (TAPS, TAPS), 0)
    target = lax.broadcasted_iota(jnp.int32, (TAPS, TAPS), 1)
    turn = jnp.where((source + target) % TAPS == 0, 1.0, 0.0)
    return jnp.dot(sums, turn, precision=lax.Precision.HIGHEST, preferred_element_type=jnp.float32)


def tile_of(index):
    return slice(index * LANES, (index + 1) * LANES), slice(index * PER * HALF, (index + 1) * PER * HALF)


def main_kernel(place_ref, earlier_lo_ref, earlier_hi_ref, cur_ref, grad_ref, later_lo_ref, later_hi_ref, fwd_ref, bwd_ref, skip_ref, conv_ref, back_ref, lag_ref, diag_ref):
    lower = pl.program_id(0) == 0

    for at_end, forward, own_ref, halo_refs, matrix_ref, out_ref in (
        (0, True, cur_ref, (earlier_lo_ref, earlier_hi_ref), fwd_ref, conv_ref),
        (ROW - 1, False, grad_ref, (later_lo_ref, later_hi_ref), bwd_ref, back_ref),
    ):

        @pl.when(place_ref[0] != at_end)
        def _():
            mask = inside_mask(forward)
            for index in range(MAIN_TILES):
                lanes, rows = tile_of(index)
                own = own_ref[:, lanes]
                halo = jnp.where(lower, halo_refs[0][:, lanes], halo_refs[1][:, lanes])
                out_ref[:, lanes] = convolved(forward, matrix_ref[0, rows], mask, own, halo, skip_ref[:, lanes])

    sums = []
    for index in range(MAIN_TILES):
        lanes, _ = tile_of(index)
        cur, grad = cur_ref[:, lanes], grad_ref[:, lanes]
        earlier = jnp.where(lower, earlier_lo_ref[:, lanes], earlier_hi_ref[:, lanes])
        diag_ref[:, lanes] = jnp.sum(cur.astype(jnp.float32) * grad.astype(jnp.float32), axis=0, keepdims=True)
        sums.append(cross_sums(earlier, cur, grad))
    lag_ref[...] = by_lag(jnp.concatenate(sums, axis=0))


def main_part(place, earlier, cur, grad, later, matrices, skip):
    tokens, chans = cur.shape
    spec = pl.BlockSpec((tokens, MAIN_WIDE), lambda i, place: (0, i))
    half = pl.BlockSpec((tokens, MAIN_WIDE), lambda i, place: (0, 0))
    row_spec = pl.BlockSpec((1, MAIN_WIDE), lambda i, place: (0, i))
    narrow = jax.ShapeDtypeStruct((tokens, chans), jnp.bfloat16)
    return pl.pallas_call(
        main_kernel,
        grid_spec=pltpu.PrefetchScalarGridSpec(
            num_scalar_prefetch=1,
            grid=(chans // MAIN_WIDE,),
            in_specs=[half, half, spec, spec, half, half]
            + [
                pl.BlockSpec((1, MAIN_TILES * PER * HALF, TAPS), lambda i, place: (0, i, 0)),
                pl.BlockSpec((1, MAIN_TILES * PER * HALF, TAPS), lambda i, place: (1, i, 0)),
                row_spec,
            ],
            out_specs=[spec, spec, pl.BlockSpec((MAIN_TILES * PER, TAPS), lambda i, place: (i, 0)), row_spec],
        ),
        out_shape=[
            narrow,
            narrow,
            jax.ShapeDtypeStruct((chans // CH, TAPS), jnp.float32),
            jax.ShapeDtypeStruct((1, chans), jnp.float32),
        ],
        compiler_params=params(40 * 1024 * 1024),
        cost_estimate=SHORT,
        name="main_part",
    )(place, *earlier, cur, grad, *later, matrices, matrices, skip)


def far_fix_kernel(place_ref, halo_ref, cur_ref, grad_ref, matrix_ref, fwd_skip_ref, bwd_skip_ref, conv_ref, back_ref, *refs):
    if len(refs) == 2:
        conv_out_ref, back_out_ref = refs
    else:
        fwd_values_ref, bwd_grads_ref, lag_ref, conv_out_ref, back_out_ref, lag_out_ref = refs
    place = place_ref[0]

    def added(earlier_ref, own_ref):
        sums = []
        for index in range(TILES):
            lanes, _ = tile_of(index)
            earlier = earlier_ref[:, lanes]
            sums.append(cross_sums(earlier, jnp.zeros_like(earlier), own_ref[:, lanes]))
        lag_out_ref[...] = lag_ref[...] + by_lag(jnp.concatenate(sums, axis=0))

    def redo(forward, own_ref, skip_ref, out_ref):
        mask = inside_mask(forward)
        for index in range(TILES):
            lanes, rows = tile_of(index)
            own, halo = own_ref[:, lanes], halo_ref[:, lanes]
            out_ref[:, lanes] = convolved(forward, matrix_ref[0, rows], mask, own, halo, skip_ref[:, lanes])

    @pl.when(place == 0)
    def _():
        redo(True, cur_ref, fwd_skip_ref, conv_out_ref)
        if len(refs) != 2:
            added(halo_ref, fwd_values_ref)

    @pl.when(place != 0)
    def _():
        conv_out_ref[...] = conv_ref[...]

    @pl.when(place == ROW - 1)
    def _():
        redo(False, grad_ref, bwd_skip_ref, back_out_ref)
        if len(refs) != 2:
            added(bwd_grads_ref, halo_ref)

    @pl.when(place != ROW - 1)
    def _():
        back_out_ref[...] = back_ref[...]

    if len(refs) != 2:

        @pl.when((place != 0) & (place != ROW - 1))
        def _():
            lag_out_ref[...] = lag_ref[...]


def far_fix(place, halo, cur, grad, matrices, skip, conv, back, lagged=None):
    tokens, chans = cur.shape
    steps = chans // WIDE // 2
    fwd_at, bwd_at = (steps, 0) if lagged is None else (0, steps)
    fwd_spec = pl.BlockSpec((tokens, WIDE), lambda i, place: (0, fwd_at + i))
    bwd_spec = pl.BlockSpec((tokens, WIDE), lambda i, place: (0, bwd_at + i))

    def part(i, place):
        return jnp.where(place[0] == ROW - 1, bwd_at, fwd_at) + i

    in_specs = [
        pl.BlockSpec((tokens, WIDE), lambda i, place: (0, i)),
        fwd_spec,
        bwd_spec,
        pl.BlockSpec(
            (1, TILES * PER * HALF, TAPS),
            lambda i, place: (jnp.where(place[0] == ROW - 1, 1, 0), part(i, place), 0),
        ),
        pl.BlockSpec((1, WIDE), lambda i, place: (0, fwd_at + i)),
        pl.BlockSpec((1, WIDE), lambda i, place: (0, bwd_at + i)),
        fwd_spec,
        bwd_spec,
    ]
    out_specs = [fwd_spec, bwd_spec]
    out_shape = [jax.ShapeDtypeStruct((tokens, chans), jnp.bfloat16)] * 2
    aliases = {7: 0, 8: 1}
    args = [place, halo, cur, grad, matrices, skip, skip, conv, back]
    if lagged is not None:
        lag_spec = pl.BlockSpec((TILES * PER, TAPS), lambda i, place: (part(i, place), 0))
        in_specs += [fwd_spec, bwd_spec, lag_spec]
        out_specs += [lag_spec]
        out_shape += [jax.ShapeDtypeStruct(lagged.shape, jnp.float32)]
        aliases[11] = 2
        args += [grad, cur, lagged]
    return pl.pallas_call(
        far_fix_kernel,
        grid_spec=pltpu.PrefetchScalarGridSpec(
            num_scalar_prefetch=1, grid=(steps,), in_specs=in_specs, out_specs=out_specs
        ),
        out_shape=out_shape,
        input_output_aliases=aliases,
        compiler_params=params(LARGE if lagged is None else SMALL),
        cost_estimate=SHORT,
        name="late_fix" if lagged is None else "early_fix",
    )(*args)


def over_plane(lagged, diagonal):
    ctx, dp = lax.axis_size("ctx"), lax.axis_size("dp")
    pairs = [[y * 2 * ROW + z * ROW + x for y in range(ctx // ROW // 2) for x in range(ROW)] for z in range(2)]
    sent = jnp.concatenate([lagged.reshape(ctx, -1), diagonal.reshape(ctx, -1)], axis=1)
    sent = sent.reshape(-1, 2, ROW, sent.shape[1]).transpose(0, 2, 1, 3).reshape(ctx // 2, -1)
    got = jnp.sum(lax.all_to_all(sent, "ctx", 0, 0, axis_index_groups=pairs, tiled=True), axis=0).reshape(2, -1)
    groups = lagged.shape[0] // ctx
    taps = got[:, : groups * TAPS].reshape(2, groups, dp, TAPS // dp).transpose(0, 2, 1, 3).reshape(2 * dp, -1)
    return jnp.concatenate([taps, got[:, groups * TAPS :].reshape(2 * dp, -1)], axis=1)


def over_column(sent):
    ctx, dp = lax.axis_size("ctx"), lax.axis_size("dp")
    columns = [
        [d * ctx + y * 2 * ROW + z * ROW + x for z in range(2) for d in range(dp)]
        for y in range(ctx // ROW // 2)
        for x in range(ROW)
    ]
    return jnp.sum(lax.all_to_all(sent, ("dp", "ctx"), 0, 0, axis_index_groups=columns, tiled=True), axis=0)


def in_order(step, *arrays):
    there = lax.axis_index("ctx") < lax.axis_size("ctx")
    shapes = jax.eval_shape(step, *arrays)
    nothing = lambda *_: jax.tree.map(lambda shape: jnp.zeros(shape.shape, shape.dtype), shapes)
    return lax.cond(there, step, nothing, *arrays)


def permuted(array, pairs):
    return lax.ppermute(array, "ctx", pairs)


def shards(features, cotangent, filters, skip_gain):
    ctx = lax.axis_size("ctx")
    token_total = lax.axis_size("dp") * features.shape[0] * features.shape[1] * ctx
    cur, grad = features[0], cotangent[0]
    skip = skip_gain.reshape(1, -1)
    half = cur.shape[1] // 2
    x = lax.axis_index("ctx") % ROW
    place = x.astype(jnp.int32).reshape(1)
    near = [i for i in range(ctx - 1) if i % ROW != ROW - 1]
    far = [i for i in range(ctx - 1) if i % ROW == ROW - 1]
    straight = [(i, i + 1) for i in far] + [(i + 1, i) for i in far]
    aside = [(i, i - 1) for i in far] + [(i + 1, i + 2) for i in far]
    onward = [(i - 1, i + 2) for i in far] + [(i + 2, i - 1) for i in far]
    home = [(i + 2, i + 1) for i in far] + [(i - 1, i) for i in far]

    last = x == ROW - 1
    early = jnp.where(last, cur[:, :half], grad[:, half:])
    late = jnp.where(last, cur[:, half:], grad[:, :half])
    early, late, filters = lax.optimization_barrier((early, late, filters))
    early = permuted(early, straight)
    late = permuted(late, aside)
    halves = slice(0, half), slice(half, 2 * half)
    earlier = [permuted(cur[:, lanes], [(i, i + 1) for i in near]) for lanes in halves]
    later = [permuted(grad[:, lanes], [(i + 1, i) for i in near]) for lanes in halves]
    matrices = circulants(filters)
    late = permuted(jnp.where((x == 0) | last, jnp.zeros_like(late), late), onward)
    conv, back, lagged, diagonal = main_part(place, earlier, cur, grad, later, matrices, skip)
    early, lagged = lax.optimization_barrier((early, lagged))
    conv, back, lagged = far_fix(place, early, cur, grad, matrices, skip, conv, back, lagged)
    sent = in_order(over_plane, lagged, diagonal)
    late, sent = lax.optimization_barrier((late, sent))
    late = permuted(late, home)
    sums = in_order(over_column, sent)
    conv, back = far_fix(place, late, cur, grad, matrices, skip, conv, back)
    cut = sums.shape[0] - cur.shape[1] // (ctx * lax.axis_size("dp"))
    grad_filters = sums[:cut].reshape(-1, TAPS // lax.axis_size("dp")) / math.sqrt(token_total * CH)
    grad_skip = sums[cut:] / math.sqrt(token_total)
    return (conv[None], back[None], grad_filters, grad_skip)


def solution(mesh):
    return jax.shard_map(
        shards,
        mesh=mesh,
        in_specs=(P("dp", "ctx", None), P("dp", "ctx", None), P(), P()),
        out_specs=(P("dp", "ctx", None), P("dp", "ctx", None), P("ctx", "dp"), P(("ctx", "dp"))),
        check_vma=False,
    )
```

```python
import functools
import math

import jax
import jax.numpy as jnp
from jax import lax
from jax.experimental import pallas as pl
from jax.experimental.pallas import tpu as pltpu
from jax.sharding import PartitionSpec as P

CH = 16
TAPS = 128
LANES = 128
PER = LANES // CH
HALF = 64
QUARTER = 32
TILES = 8
WIDE = TILES * LANES
MAIN_TILES = 16
MAIN_WIDE = MAIN_TILES * LANES
ROW = 4
LARGE, SMALL = 51 * 1024 * 1024, 24 * 1024 * 1024
SHORT = pl.CostEstimate(flops=1, bytes_accessed=1, transcendentals=0)


def params(limit=SMALL):
    return pltpu.CompilerParams(vmem_limit_bytes=limit)


def circulant_kernel(taps_ref, out_ref):
    taps = taps_ref[...]
    groups = taps.shape[0]
    source = lax.broadcasted_iota(jnp.int32, (TAPS, TAPS), 0)
    target = lax.broadcasted_iota(jnp.int32, (TAPS, TAPS), 1)
    turn = jnp.where((source + target) % TAPS == 0, 1.0, 0.0).astype(jnp.bfloat16)
    back = jnp.dot(taps, turn, preferred_element_type=jnp.float32)
    for way, rows in enumerate((back, taps.astype(jnp.float32))):
        first = [
            pltpu.roll(jnp.broadcast_to(rows[g : g + 1], (8, TAPS)), 0, 1, stride=1, stride_axis=0)
            for g in range(groups)
        ]
        first = jnp.concatenate(first, axis=0)
        for pair in range(HALF // 16):
            low = pltpu.roll(first, pair * 16, 1) if pair else first
            high = pltpu.roll(first, pair * 16 + 8, 1)
            both = jnp.concatenate([low.reshape(groups, 8, TAPS), high.reshape(groups, 8, TAPS)], axis=1)
            out_ref[way, :, pair * 16 : pair * 16 + 16, :] = both.astype(jnp.bfloat16)


def circulants(filters):
    groups = filters.shape[0]
    step = 64
    out = pl.pallas_call(
        circulant_kernel,
        grid=(groups // step,),
        in_specs=[pl.BlockSpec((step, TAPS), lambda i: (i, 0))],
        out_specs=pl.BlockSpec((2, step, HALF, TAPS), lambda i: (0, i, 0, 0)),
        out_shape=jax.ShapeDtypeStruct((2, groups, HALF, TAPS), jnp.bfloat16),
        compiler_params=params(),
        cost_estimate=SHORT,
        name="circulants",
    )(filters)
    return out.reshape(2, groups * HALF, TAPS)


def inside_mask(forward):
    row = lax.broadcasted_iota(jnp.int32, (PER * HALF, TAPS), 0) % HALF
    lane = lax.broadcasted_iota(jnp.int32, (PER * HALF, TAPS), 1)
    kept = (lane <= row) | (lane >= HALF) if forward else lane >= row
    return jnp.where(kept, 1.0, 0.0).astype(jnp.bfloat16)


def picked(product):
    lane = lax.broadcasted_iota(jnp.int32, (HALF, 2 * LANES), 1)
    owner = (lane % LANES) // CH
    kept = product[:HALF]
    for group in range(1, PER):
        kept = jnp.where(owner == group, product[group * HALF : (group + 1) * HALF], kept)
    return jnp.concatenate([kept[:, :LANES], kept[:, LANES:]], axis=0)


def convolved(forward, matrix, mask, own, halo, skip):
    inside = matrix * mask
    both = jnp.concatenate([inside, matrix - inside], axis=1)
    none = jnp.zeros_like(own[:HALF])
    if forward:
        left = [own[:HALF], halo[HALF:], halo[:HALF], none]
        right = [own[HALF:], own[:HALF], halo[HALF:], none]
    else:
        left = [own, halo[:HALF], none]
        right = [own[HALF:], halo[:HALF], halo[HALF:], none]
    window = jnp.concatenate([jnp.concatenate(left, axis=0), jnp.concatenate(right, axis=0)], axis=1)
    total = picked(jnp.dot(both, window, preferred_element_type=jnp.float32))
    return (total + skip * own.astype(jnp.float32)).astype(jnp.bfloat16)


def cross_sums(earlier, cur, grad):
    both = jnp.concatenate([earlier, cur], axis=0)
    span = QUARTER + TAPS
    blocks = TAPS // QUARTER
    values = jnp.concatenate([both[b * QUARTER : b * QUARTER + span] for b in range(blocks)], axis=1)
    grads = jnp.concatenate([grad[b * QUARTER : (b + 1) * QUARTER] for b in range(blocks)], axis=1)
    lane = lax.broadcasted_iota(jnp.int32, grads.shape, 1)
    owner = (lane % LANES) // CH
    zero = jnp.zeros_like(grads)
    masked = jnp.concatenate([jnp.where(owner == group, grads, zero) for group in range(PER)], axis=0)
    cross = lax.dot_general(masked, values, (((1,), (1,)), ((), ())), preferred_element_type=jnp.float32)
    rest = jnp.concatenate([cross[:, TAPS:], jnp.zeros((cross.shape[0], 2 * TAPS - span), jnp.float32)], axis=1)
    row = lax.broadcasted_iota(jnp.int32, rest.shape, 0) % QUARTER
    folded = jnp.where(lax.broadcasted_iota(jnp.int32, rest.shape, 1) > row, cross[:, :TAPS], rest)
    rows = 8
    parts = folded.reshape(PER, QUARTER // rows, rows, TAPS)
    total = parts[:, 0].reshape(PER * rows, TAPS)
    for part in range(1, QUARTER // rows):
        total = total + pltpu.roll(parts[:, part].reshape(PER * rows, TAPS), TAPS - part * rows, 1)
    row = lax.broadcasted_iota(jnp.int32, total.shape, 0) % rows
    for bit in (1, 2, 4):
        total = jnp.where(row & bit != 0, pltpu.roll(total, TAPS - bit, 1), total)
    return jnp.sum(total.reshape(PER, rows, TAPS), axis=1)


def by_lag(sums):
    source = lax.broadcasted_iota(jnp.int32, (TAPS, TAPS), 0)
    target = lax.broadcasted_iota(jnp.int32, (TAPS, TAPS), 1)
    turn = jnp.where((source + target) % TAPS == 0, 1.0, 0.0)
    return jnp.dot(sums, turn, precision=lax.Precision.HIGHEST, preferred_element_type=jnp.float32)


def tile_of(index):
    return slice(index * LANES, (index + 1) * LANES), slice(index * PER * HALF, (index + 1) * PER * HALF)


def main_kernel(place_ref, earlier_lo_ref, earlier_hi_ref, cur_ref, grad_ref, later_lo_ref, later_hi_ref, fwd_ref, bwd_ref, skip_ref, conv_ref, back_ref, lag_ref, diag_ref):
    lower = pl.program_id(0) == 0

    for at_end, forward, own_ref, halo_refs, matrix_ref, out_ref in (
        (0, True, cur_ref, (earlier_lo_ref, earlier_hi_ref), fwd_ref, conv_ref),
        (ROW - 1, False, grad_ref, (later_lo_ref, later_hi_ref), bwd_ref, back_ref),
    ):

        @pl.when(place_ref[0] != at_end)
        def _():
            mask = inside_mask(forward)
            for index in range(MAIN_TILES):
                lanes, rows = tile_of(index)
                own = own_ref[:, lanes]
                halo = jnp.where(lower, halo_refs[0][:, lanes], halo_refs[1][:, lanes])
                out_ref[:, lanes] = convolved(forward, matrix_ref[0, rows], mask, own, halo, skip_ref[:, lanes])

    sums = []
    for index in range(MAIN_TILES):
        lanes, _ = tile_of(index)
        cur, grad = cur_ref[:, lanes], grad_ref[:, lanes]
        earlier = jnp.where(lower, earlier_lo_ref[:, lanes], earlier_hi_ref[:, lanes])
        diag_ref[:, lanes] = jnp.sum(cur.astype(jnp.float32) * grad.astype(jnp.float32), axis=0, keepdims=True)
        sums.append(cross_sums(earlier, cur, grad))
    lag_ref[...] = by_lag(jnp.concatenate(sums, axis=0))


def main_part(place, earlier, cur, grad, later, matrices, skip):
    tokens, chans = cur.shape
    spec = pl.BlockSpec((tokens, MAIN_WIDE), lambda i, place: (0, i))
    half = pl.BlockSpec((tokens, MAIN_WIDE), lambda i, place: (0, 0))
    row_spec = pl.BlockSpec((1, MAIN_WIDE), lambda i, place: (0, i))
    narrow = jax.ShapeDtypeStruct((tokens, chans), jnp.bfloat16)
    return pl.pallas_call(
        main_kernel,
        grid_spec=pltpu.PrefetchScalarGridSpec(
            num_scalar_prefetch=1,
            grid=(chans // MAIN_WIDE,),
            in_specs=[half, half, spec, spec, half, half]
            + [
                pl.BlockSpec((1, MAIN_TILES * PER * HALF, TAPS), lambda i, place: (0, i, 0)),
                pl.BlockSpec((1, MAIN_TILES * PER * HALF, TAPS), lambda i, place: (1, i, 0)),
                row_spec,
            ],
            out_specs=[spec, spec, pl.BlockSpec((MAIN_TILES * PER, TAPS), lambda i, place: (i, 0)), row_spec],
        ),
        out_shape=[
            narrow,
            narrow,
            jax.ShapeDtypeStruct((chans // CH, TAPS), jnp.float32),
            jax.ShapeDtypeStruct((1, chans), jnp.float32),
        ],
        compiler_params=params(40 * 1024 * 1024),
        cost_estimate=SHORT,
        name="main_part",
    )(place, *earlier, cur, grad, *later, matrices, matrices, skip)


def far_fix_kernel(place_ref, halo_ref, cur_ref, grad_ref, matrix_ref, fwd_skip_ref, bwd_skip_ref, conv_ref, back_ref, *refs):
    if len(refs) == 2:
        conv_out_ref, back_out_ref = refs
    else:
        fwd_values_ref, bwd_grads_ref, lag_ref, conv_out_ref, back_out_ref, lag_out_ref = refs
    place = place_ref[0]

    def added(earlier_ref, own_ref):
        sums = []
        for index in range(TILES):
            lanes, _ = tile_of(index)
            earlier = earlier_ref[:, lanes]
            sums.append(cross_sums(earlier, jnp.zeros_like(earlier), own_ref[:, lanes]))
        lag_out_ref[...] = lag_ref[...] + by_lag(jnp.concatenate(sums, axis=0))

    def redo(forward, own_ref, skip_ref, out_ref):
        mask = inside_mask(forward)
        for index in range(TILES):
            lanes, rows = tile_of(index)
            own, halo = own_ref[:, lanes], halo_ref[:, lanes]
            out_ref[:, lanes] = convolved(forward, matrix_ref[0, rows], mask, own, halo, skip_ref[:, lanes])

    @pl.when(place == 0)
    def _():
        redo(True, cur_ref, fwd_skip_ref, conv_out_ref)
        if len(refs) != 2:
            added(halo_ref, fwd_values_ref)

    @pl.when(place != 0)
    def _():
        conv_out_ref[...] = conv_ref[...]

    @pl.when(place == ROW - 1)
    def _():
        redo(False, grad_ref, bwd_skip_ref, back_out_ref)
        if len(refs) != 2:
            added(bwd_grads_ref, halo_ref)

    @pl.when(place != ROW - 1)
    def _():
        back_out_ref[...] = back_ref[...]

    if len(refs) != 2:

        @pl.when((place != 0) & (place != ROW - 1))
        def _():
            lag_out_ref[...] = lag_ref[...]


def far_fix(place, halo, cur, grad, matrices, skip, conv, back, lagged=None):
    tokens, chans = cur.shape
    steps = chans // WIDE // 2
    fwd_at, bwd_at = (steps, 0) if lagged is None else (0, steps)
    fwd_spec = pl.BlockSpec((tokens, WIDE), lambda i, place: (0, fwd_at + i))
    bwd_spec = pl.BlockSpec((tokens, WIDE), lambda i, place: (0, bwd_at + i))

    def part(i, place):
        return jnp.where(place[0] == ROW - 1, bwd_at, fwd_at) + i

    in_specs = [
        pl.BlockSpec((tokens, WIDE), lambda i, place: (0, i)),
        fwd_spec,
        bwd_spec,
        pl.BlockSpec(
            (1, TILES * PER * HALF, TAPS),
            lambda i, place: (jnp.where(place[0] == ROW - 1, 1, 0), part(i, place), 0),
        ),
        pl.BlockSpec((1, WIDE), lambda i, place: (0, fwd_at + i)),
        pl.BlockSpec((1, WIDE), lambda i, place: (0, bwd_at + i)),
        fwd_spec,
        bwd_spec,
    ]
    out_specs = [fwd_spec, bwd_spec]
    out_shape = [jax.ShapeDtypeStruct((tokens, chans), jnp.bfloat16)] * 2
    aliases = {7: 0, 8: 1}
    args = [place, halo, cur, grad, matrices, skip, skip, conv, back]
    if lagged is not None:
        lag_spec = pl.BlockSpec((TILES * PER, TAPS), lambda i, place: (part(i, place), 0))
        in_specs += [fwd_spec, bwd_spec, lag_spec]
        out_specs += [lag_spec]
        out_shape += [jax.ShapeDtypeStruct(lagged.shape, jnp.float32)]
        aliases[11] = 2
        args += [grad, cur, lagged]
    return pl.pallas_call(
        far_fix_kernel,
        grid_spec=pltpu.PrefetchScalarGridSpec(
            num_scalar_prefetch=1, grid=(steps,), in_specs=in_specs, out_specs=out_specs
        ),
        out_shape=out_shape,
        input_output_aliases=aliases,
        compiler_params=params(LARGE if lagged is None else SMALL),
        cost_estimate=SHORT,
        name="late_fix" if lagged is None else "early_fix",
    )(*args)


def over_plane(lagged, diagonal):
    ctx, dp = lax.axis_size("ctx"), lax.axis_size("dp")
    pairs = [[y * 2 * ROW + z * ROW + x for y in range(ctx // ROW // 2) for x in range(ROW)] for z in range(2)]
    sent = jnp.concatenate([lagged.reshape(ctx, -1), diagonal.reshape(ctx, -1)], axis=1)
    sent = sent.reshape(-1, 2, ROW, sent.shape[1]).transpose(0, 2, 1, 3).reshape(ctx // 2, -1)
    got = jnp.sum(lax.all_to_all(sent, "ctx", 0, 0, axis_index_groups=pairs, tiled=True), axis=0).reshape(2, -1)
    groups = lagged.shape[0] // ctx
    taps = got[:, : groups * TAPS].reshape(2, groups, dp, TAPS // dp).transpose(0, 2, 1, 3).reshape(2 * dp, -1)
    return jnp.concatenate([taps, got[:, groups * TAPS :].reshape(2 * dp, -1)], axis=1)


def over_column(sent):
    ctx, dp = lax.axis_size("ctx"), lax.axis_size("dp")
    columns = [
        [d * ctx + y * 2 * ROW + z * ROW + x for z in range(2) for d in range(dp)]
        for y in range(ctx // ROW // 2)
        for x in range(ROW)
    ]
    return jnp.sum(lax.all_to_all(sent, ("dp", "ctx"), 0, 0, axis_index_groups=columns, tiled=True), axis=0)


def in_order(step, *arrays):
    there = lax.axis_index("ctx") < lax.axis_size("ctx")
    shapes = jax.eval_shape(step, *arrays)
    nothing = lambda *_: jax.tree.map(lambda shape: jnp.zeros(shape.shape, shape.dtype), shapes)
    return lax.cond(there, step, nothing, *arrays)


def permuted(array, pairs):
    return lax.ppermute(array, "ctx", pairs)


def shards(features, cotangent, filters, skip_gain):
    ctx = lax.axis_size("ctx")
    token_total = lax.axis_size("dp") * features.shape[0] * features.shape[1] * ctx
    cur, grad = features[0], cotangent[0]
    skip = skip_gain.reshape(1, -1)
    half = cur.shape[1] // 2
    x = lax.axis_index("ctx") % ROW
    place = x.astype(jnp.int32).reshape(1)
    near = [i for i in range(ctx - 1) if i % ROW != ROW - 1]
    far = [i for i in range(ctx - 1) if i % ROW == ROW - 1]
    straight = [(i, i + 1) for i in far] + [(i + 1, i) for i in far]
    aside = [(i, i - 1) for i in far] + [(i + 1, i + 2) for i in far]
    onward = [(i - 1, i + 2) for i in far] + [(i + 2, i - 1) for i in far]
    home = [(i + 2, i + 1) for i in far] + [(i - 1, i) for i in far]

    last = x == ROW - 1
    early = jnp.where(last, cur[:, :half], grad[:, half:])
    late = jnp.where(last, cur[:, half:], grad[:, :half])
    early, late, filters = lax.optimization_barrier((early, late, filters))
    early = permuted(early, straight)
    late = permuted(late, aside)
    halves = slice(0, half), slice(half, 2 * half)
    earlier = [permuted(cur[:, lanes], [(i, i + 1) for i in near]) for lanes in halves]
    later = [permuted(grad[:, lanes], [(i + 1, i) for i in near]) for lanes in halves]
    matrices = circulants(filters)
    late = lax.optimization_barrier(jnp.where((x == 0) | last, jnp.zeros_like(late), late))
    late = permuted(jnp.where((x == 0) | last, jnp.zeros_like(late), late), onward)
    conv, back, lagged, diagonal = main_part(place, earlier, cur, grad, later, matrices, skip)
    early, lagged = lax.optimization_barrier((early, lagged))
    conv, back, lagged = far_fix(place, early, cur, grad, matrices, skip, conv, back, lagged)
    sent = in_order(over_plane, lagged, diagonal)
    late, sent = lax.optimization_barrier((late, sent))
    late = permuted(late, home)
    sums = in_order(over_column, sent)
    conv, back = far_fix(place, late, cur, grad, matrices, skip, conv, back)
    cut = sums.shape[0] - cur.shape[1] // (ctx * lax.axis_size("dp"))
    grad_filters = sums[:cut].reshape(-1, TAPS // lax.axis_size("dp")) / math.sqrt(token_total * CH)
    grad_skip = sums[cut:] / math.sqrt(token_total)
    return (conv[None], back[None], grad_filters, grad_skip)


def solution(mesh):
    return jax.shard_map(
        shards,
        mesh=mesh,
        in_specs=(P("dp", "ctx", None), P("dp", "ctx", None), P(), P()),
        out_specs=(P("dp", "ctx", None), P("dp", "ctx", None), P("ctx", "dp"), P(("ctx", "dp"))),
        check_vma=False,
    )
```

```python
import functools
import math

import jax
import jax.numpy as jnp
from jax import lax
from jax.experimental import pallas as pl
from jax.experimental.pallas import tpu as pltpu
from jax.sharding import PartitionSpec as P

CH = 16
TAPS = 128
LANES = 128
PER = LANES // CH
HALF = 64
QUARTER = 32
TILES = 8
WIDE = TILES * LANES
MAIN_TILES = 16
MAIN_WIDE = MAIN_TILES * LANES
ROW = 4
LARGE, SMALL = 51 * 1024 * 1024, 24 * 1024 * 1024
SHORT = pl.CostEstimate(flops=1, bytes_accessed=1, transcendentals=0)


def params(limit=SMALL):
    return pltpu.CompilerParams(vmem_limit_bytes=limit)


def circulant_kernel(taps_ref, out_ref):
    taps = taps_ref[...]
    groups = taps.shape[0]
    source = lax.broadcasted_iota(jnp.int32, (TAPS, TAPS), 0)
    target = lax.broadcasted_iota(jnp.int32, (TAPS, TAPS), 1)
    turn = jnp.where((source + target) % TAPS == 0, 1.0, 0.0).astype(jnp.bfloat16)
    back = jnp.dot(taps, turn, preferred_element_type=jnp.float32)
    for way, rows in enumerate((back, taps.astype(jnp.float32))):
        first = [
            pltpu.roll(jnp.broadcast_to(rows[g : g + 1], (8, TAPS)), 0, 1, stride=1, stride_axis=0)
            for g in range(groups)
        ]
        first = jnp.concatenate(first, axis=0)
        for pair in range(HALF // 16):
            low = pltpu.roll(first, pair * 16, 1) if pair else first
            high = pltpu.roll(first, pair * 16 + 8, 1)
            both = jnp.concatenate([low.reshape(groups, 8, TAPS), high.reshape(groups, 8, TAPS)], axis=1)
            out_ref[way, :, pair * 16 : pair * 16 + 16, :] = both.astype(jnp.bfloat16)


def circulants(filters):
    groups = filters.shape[0]
    step = 64
    out = pl.pallas_call(
        circulant_kernel,
        grid=(groups // step,),
        in_specs=[pl.BlockSpec((step, TAPS), lambda i: (i, 0))],
        out_specs=pl.BlockSpec((2, step, HALF, TAPS), lambda i: (0, i, 0, 0)),
        out_shape=jax.ShapeDtypeStruct((2, groups, HALF, TAPS), jnp.bfloat16),
        compiler_params=params(),
        cost_estimate=SHORT,
        name="circulants",
    )(filters)
    return out.reshape(2, groups * HALF, TAPS)


def inside_mask(forward):
    row = lax.broadcasted_iota(jnp.int32, (PER * HALF, TAPS), 0) % HALF
    lane = lax.broadcasted_iota(jnp.int32, (PER * HALF, TAPS), 1)
    kept = (lane <= row) | (lane >= HALF) if forward else lane >= row
    return jnp.where(kept, 1.0, 0.0).astype(jnp.bfloat16)


def picked(product):
    lane = lax.broadcasted_iota(jnp.int32, (HALF, 2 * LANES), 1)
    owner = (lane % LANES) // CH
    kept = product[:HALF]
    for group in range(1, PER):
        kept = jnp.where(owner == group, product[group * HALF : (group + 1) * HALF], kept)
    return jnp.concatenate([kept[:, :LANES], kept[:, LANES:]], axis=0)


def convolved(forward, matrix, mask, own, halo, skip):
    inside = matrix * mask
    both = jnp.concatenate([inside, matrix - inside], axis=1)
    none = jnp.zeros_like(own[:HALF])
    if forward:
        left = [own[:HALF], halo[HALF:], halo[:HALF], none]
        right = [own[HALF:], own[:HALF], halo[HALF:], none]
    else:
        left = [own, halo[:HALF], none]
        right = [own[HALF:], halo[:HALF], halo[HALF:], none]
    window = jnp.concatenate([jnp.concatenate(left, axis=0), jnp.concatenate(right, axis=0)], axis=1)
    total = picked(jnp.dot(both, window, preferred_element_type=jnp.float32))
    return (total + skip * own.astype(jnp.float32)).astype(jnp.bfloat16)


def cross_sums(earlier, cur, grad):
    both = jnp.concatenate([earlier, cur], axis=0)
    span = QUARTER + TAPS
    blocks = TAPS // QUARTER
    values = jnp.concatenate([both[b * QUARTER : b * QUARTER + span] for b in range(blocks)], axis=1)
    grads = jnp.concatenate([grad[b * QUARTER : (b + 1) * QUARTER] for b in range(blocks)], axis=1)
    lane = lax.broadcasted_iota(jnp.int32, grads.shape, 1)
    owner = (lane % LANES) // CH
    zero = jnp.zeros_like(grads)
    masked = jnp.concatenate([jnp.where(owner == group, grads, zero) for group in range(PER)], axis=0)
    cross = lax.dot_general(masked, values, (((1,), (1,)), ((), ())), preferred_element_type=jnp.float32)
    rest = jnp.concatenate([cross[:, TAPS:], jnp.zeros((cross.shape[0], 2 * TAPS - span), jnp.float32)], axis=1)
    row = lax.broadcasted_iota(jnp.int32, rest.shape, 0) % QUARTER
    folded = jnp.where(lax.broadcasted_iota(jnp.int32, rest.shape, 1) > row, cross[:, :TAPS], rest)
    rows = 8
    parts = folded.reshape(PER, QUARTER // rows, rows, TAPS)
    total = parts[:, 0].reshape(PER * rows, TAPS)
    for part in range(1, QUARTER // rows):
        total = total + pltpu.roll(parts[:, part].reshape(PER * rows, TAPS), TAPS - part * rows, 1)
    row = lax.broadcasted_iota(jnp.int32, total.shape, 0) % rows
    for bit in (1, 2, 4):
        total = jnp.where(row & bit != 0, pltpu.roll(total, TAPS - bit, 1), total)
    return jnp.sum(total.reshape(PER, rows, TAPS), axis=1)


def by_lag(sums):
    source = lax.broadcasted_iota(jnp.int32, (TAPS, TAPS), 0)
    target = lax.broadcasted_iota(jnp.int32, (TAPS, TAPS), 1)
    turn = jnp.where((source + target) % TAPS == 0, 1.0, 0.0)
    return jnp.dot(sums, turn, precision=lax.Precision.HIGHEST, preferred_element_type=jnp.float32)


def tile_of(index):
    return slice(index * LANES, (index + 1) * LANES), slice(index * PER * HALF, (index + 1) * PER * HALF)


def main_kernel(place_ref, earlier_lo_ref, earlier_hi_ref, cur_ref, grad_ref, later_lo_ref, later_hi_ref, fwd_ref, bwd_ref, skip_ref, conv_ref, back_ref, lag_ref, diag_ref):
    lower = pl.program_id(0) == 0

    for at_end, forward, own_ref, halo_refs, matrix_ref, out_ref in (
        (0, True, cur_ref, (earlier_lo_ref, earlier_hi_ref), fwd_ref, conv_ref),
        (ROW - 1, False, grad_ref, (later_lo_ref, later_hi_ref), bwd_ref, back_ref),
    ):

        @pl.when(place_ref[0] != at_end)
        def _():
            mask = inside_mask(forward)
            for index in range(MAIN_TILES):
                lanes, rows = tile_of(index)
                own = own_ref[:, lanes]
                halo = jnp.where(lower, halo_refs[0][:, lanes], halo_refs[1][:, lanes])
                out_ref[:, lanes] = convolved(forward, matrix_ref[0, rows], mask, own, halo, skip_ref[:, lanes])

    sums = []
    for index in range(MAIN_TILES):
        lanes, _ = tile_of(index)
        cur, grad = cur_ref[:, lanes], grad_ref[:, lanes]
        earlier = jnp.where(lower, earlier_lo_ref[:, lanes], earlier_hi_ref[:, lanes])
        diag_ref[:, lanes] = jnp.sum(cur.astype(jnp.float32) * grad.astype(jnp.float32), axis=0, keepdims=True)
        sums.append(cross_sums(earlier, cur, grad))
    lag_ref[...] = by_lag(jnp.concatenate(sums, axis=0))


def main_part(place, earlier, cur, grad, later, matrices, skip):
    tokens, chans = cur.shape
    spec = pl.BlockSpec((tokens, MAIN_WIDE), lambda i, place: (0, i))
    half = pl.BlockSpec((tokens, MAIN_WIDE), lambda i, place: (0, 0))
    row_spec = pl.BlockSpec((1, MAIN_WIDE), lambda i, place: (0, i))
    narrow = jax.ShapeDtypeStruct((tokens, chans), jnp.bfloat16)
    return pl.pallas_call(
        main_kernel,
        grid_spec=pltpu.PrefetchScalarGridSpec(
            num_scalar_prefetch=1,
            grid=(chans // MAIN_WIDE,),
            in_specs=[half, half, spec, spec, half, half]
            + [
                pl.BlockSpec((1, MAIN_TILES * PER * HALF, TAPS), lambda i, place: (0, i, 0)),
                pl.BlockSpec((1, MAIN_TILES * PER * HALF, TAPS), lambda i, place: (1, i, 0)),
                row_spec,
            ],
            out_specs=[spec, spec, pl.BlockSpec((MAIN_TILES * PER, TAPS), lambda i, place: (i, 0)), row_spec],
        ),
        out_shape=[
            narrow,
            narrow,
            jax.ShapeDtypeStruct((chans // CH, TAPS), jnp.float32),
            jax.ShapeDtypeStruct((1, chans), jnp.float32),
        ],
        compiler_params=params(40 * 1024 * 1024),
        cost_estimate=SHORT,
        name="main_part",
    )(place, *earlier, cur, grad, *later, matrices, matrices, skip)


def far_fix_kernel(place_ref, halo_ref, cur_ref, grad_ref, matrix_ref, fwd_skip_ref, bwd_skip_ref, conv_ref, back_ref, *refs):
    if len(refs) == 2:
        conv_out_ref, back_out_ref = refs
    else:
        fwd_values_ref, bwd_grads_ref, lag_ref, conv_out_ref, back_out_ref, lag_out_ref = refs
    place = place_ref[0]

    def added(earlier_ref, own_ref):
        sums = []
        for index in range(TILES):
            lanes, _ = tile_of(index)
            earlier = earlier_ref[:, lanes]
            sums.append(cross_sums(earlier, jnp.zeros_like(earlier), own_ref[:, lanes]))
        lag_out_ref[...] = lag_ref[...] + by_lag(jnp.concatenate(sums, axis=0))

    def redo(forward, own_ref, skip_ref, out_ref):
        mask = inside_mask(forward)
        for index in range(TILES):
            lanes, rows = tile_of(index)
            own, halo = own_ref[:, lanes], halo_ref[:, lanes]
            out_ref[:, lanes] = convolved(forward, matrix_ref[0, rows], mask, own, halo, skip_ref[:, lanes])

    @pl.when(place == 0)
    def _():
        redo(True, cur_ref, fwd_skip_ref, conv_out_ref)
        if len(refs) != 2:
            added(halo_ref, fwd_values_ref)

    @pl.when(place != 0)
    def _():
        conv_out_ref[...] = conv_ref[...]

    @pl.when(place == ROW - 1)
    def _():
        redo(False, grad_ref, bwd_skip_ref, back_out_ref)
        if len(refs) != 2:
            added(bwd_grads_ref, halo_ref)

    @pl.when(place != ROW - 1)
    def _():
        back_out_ref[...] = back_ref[...]

    if len(refs) != 2:

        @pl.when((place != 0) & (place != ROW - 1))
        def _():
            lag_out_ref[...] = lag_ref[...]


def far_fix(place, halo, cur, grad, matrices, skip, conv, back, lagged=None):
    tokens, chans = cur.shape
    steps = chans // WIDE // 2
    fwd_at, bwd_at = (steps, 0) if lagged is None else (0, steps)
    fwd_spec = pl.BlockSpec((tokens, WIDE), lambda i, place: (0, fwd_at + i))
    bwd_spec = pl.BlockSpec((tokens, WIDE), lambda i, place: (0, bwd_at + i))

    def part(i, place):
        return jnp.where(place[0] == ROW - 1, bwd_at, fwd_at) + i

    in_specs = [
        pl.BlockSpec((tokens, WIDE), lambda i, place: (0, i)),
        fwd_spec,
        bwd_spec,
        pl.BlockSpec(
            (1, TILES * PER * HALF, TAPS),
            lambda i, place: (jnp.where(place[0] == ROW - 1, 1, 0), part(i, place), 0),
        ),
        pl.BlockSpec((1, WIDE), lambda i, place: (0, fwd_at + i)),
        pl.BlockSpec((1, WIDE), lambda i, place: (0, bwd_at + i)),
        fwd_spec,
        bwd_spec,
    ]
    out_specs = [fwd_spec, bwd_spec]
    out_shape = [jax.ShapeDtypeStruct((tokens, chans), jnp.bfloat16)] * 2
    aliases = {7: 0, 8: 1}
    args = [place, halo, cur, grad, matrices, skip, skip, conv, back]
    if lagged is not None:
        lag_spec = pl.BlockSpec((TILES * PER, TAPS), lambda i, place: (part(i, place), 0))
        in_specs += [fwd_spec, bwd_spec, lag_spec]
        out_specs += [lag_spec]
        out_shape += [jax.ShapeDtypeStruct(lagged.shape, jnp.float32)]
        aliases[11] = 2
        args += [grad, cur, lagged]
    return pl.pallas_call(
        far_fix_kernel,
        grid_spec=pltpu.PrefetchScalarGridSpec(
            num_scalar_prefetch=1, grid=(steps,), in_specs=in_specs, out_specs=out_specs
        ),
        out_shape=out_shape,
        input_output_aliases=aliases,
        compiler_params=params(LARGE if lagged is None else SMALL),
        cost_estimate=SHORT,
        name="late_fix" if lagged is None else "early_fix",
    )(*args)


def over_plane(lagged, diagonal):
    ctx, dp = lax.axis_size("ctx"), lax.axis_size("dp")
    pairs = [[y * 2 * ROW + z * ROW + x for y in range(ctx // ROW // 2) for x in range(ROW)] for z in range(2)]
    sent = jnp.concatenate([lagged.reshape(ctx, -1), diagonal.reshape(ctx, -1)], axis=1)
    sent = sent.reshape(-1, 2, ROW, sent.shape[1]).transpose(0, 2, 1, 3).reshape(ctx // 2, -1)
    got = jnp.sum(lax.all_to_all(sent, "ctx", 0, 0, axis_index_groups=pairs, tiled=True), axis=0).reshape(2, -1)
    groups = lagged.shape[0] // ctx
    taps = got[:, : groups * TAPS].reshape(2, groups, dp, TAPS // dp).transpose(0, 2, 1, 3).reshape(2 * dp, -1)
    return jnp.concatenate([taps, got[:, groups * TAPS :].reshape(2 * dp, -1)], axis=1)


def over_column(sent):
    ctx, dp = lax.axis_size("ctx"), lax.axis_size("dp")
    columns = [
        [d * ctx + y * 2 * ROW + z * ROW + x for z in range(2) for d in range(dp)]
        for y in range(ctx // ROW // 2)
        for x in range(ROW)
    ]
    return jnp.sum(lax.all_to_all(sent, ("dp", "ctx"), 0, 0, axis_index_groups=columns, tiled=True), axis=0)


def in_order(step, *arrays):
    there = lax.axis_index("ctx") < lax.axis_size("ctx")
    shapes = jax.eval_shape(step, *arrays)
    nothing = lambda *_: jax.tree.map(lambda shape: jnp.zeros(shape.shape, shape.dtype), shapes)
    return lax.cond(there, step, nothing, *arrays)


def permuted(array, pairs):
    return lax.ppermute(array, "ctx", pairs)


def shards(features, cotangent, filters, skip_gain):
    ctx = lax.axis_size("ctx")
    token_total = lax.axis_size("dp") * features.shape[0] * features.shape[1] * ctx
    cur, grad = features[0], cotangent[0]
    skip = skip_gain.reshape(1, -1)
    half = cur.shape[1] // 2
    x = lax.axis_index("ctx") % ROW
    place = x.astype(jnp.int32).reshape(1)
    near = [i for i in range(ctx - 1) if i % ROW != ROW - 1]
    far = [i for i in range(ctx - 1) if i % ROW == ROW - 1]
    straight = [(i, i + 1) for i in far] + [(i + 1, i) for i in far]
    aside = [(i, i - 1) for i in far] + [(i + 1, i + 2) for i in far]
    onward = [(i - 1, i + 2) for i in far] + [(i + 2, i - 1) for i in far]
    home = [(i + 2, i + 1) for i in far] + [(i - 1, i) for i in far]

    last = x == ROW - 1
    late = jnp.where(last, cur[:, half:], grad[:, :half])
    cur_next, grad_next, late = lax.optimization_barrier((cur, grad, late))
    early = jnp.where(last, cur_next[:, :half], grad_next[:, half:])
    cur_next, grad_next, early, filters = lax.optimization_barrier((cur_next, grad_next, early, filters))
    early = permuted(early, straight)
    late = permuted(late, aside)
    halves = slice(0, half), slice(half, 2 * half)
    earlier = [permuted(cur_next[:, lanes], [(i, i + 1) for i in near]) for lanes in halves]
    later = [permuted(grad_next[:, lanes], [(i + 1, i) for i in near]) for lanes in halves]
    matrices = circulants(filters)
    late = lax.optimization_barrier(jnp.where((x == 0) | last, jnp.zeros_like(late), late))
    late = permuted(jnp.where((x == 0) | last, jnp.zeros_like(late), late), onward)
    conv, back, lagged, diagonal = main_part(place, earlier, cur, grad, later, matrices, skip)
    early, lagged = lax.optimization_barrier((early, lagged))
    conv, back, lagged = far_fix(place, early, cur, grad, matrices, skip, conv, back, lagged)
    sent = in_order(over_plane, lagged, diagonal)
    late, sent = lax.optimization_barrier((late, sent))
    late = permuted(late, home)
    sums = in_order(over_column, sent)
    conv, back = far_fix(place, late, cur, grad, matrices, skip, conv, back)
    cut = sums.shape[0] - cur.shape[1] // (ctx * lax.axis_size("dp"))
    grad_filters = sums[:cut].reshape(-1, TAPS // lax.axis_size("dp")) / math.sqrt(token_total * CH)
    grad_skip = sums[cut:] / math.sqrt(token_total)
    return (conv[None], back[None], grad_filters, grad_skip)


def solution(mesh):
    return jax.shard_map(
        shards,
        mesh=mesh,
        in_specs=(P("dp", "ctx", None), P("dp", "ctx", None), P(), P()),
        out_specs=(P("dp", "ctx", None), P("dp", "ctx", None), P("ctx", "dp"), P(("ctx", "dp"))),
        check_vma=False,
    )
```
